32 devices in a mesh: grp: 1, wide: 8 (over z, y), nar: 4 (over x, core).
Axes of the slice: x: 2, y: 2, z: 4, core: 2. Of those that a mesh axis runs over, the one named last changes fastest.
Arguments:
- tokens: bfloat16 [512, 8192], P('grp', ('nar', 'wide')), may hold values from -6 to 6
- gate_weight: bfloat16 [8192, 26624], P('nar', 'wide'), may hold values from -0.0625 to 0.0625
- gate_scale: float32 [64, 26624], P('nar', 'wide'), may hold values from 0.5 to 2
- up_weight: bfloat16 [8192, 26624], P('nar', 'wide'), may hold values from -0.0625 to 0.0625
- up_scale: float32 [64, 26624], P('nar', 'wide'), may hold values from 0.5 to 2
- down_weight: bfloat16 [26624, 8192], P('wide', 'nar'), may hold values from -0.0390625 to 0.0390625
- down_scale: float32 [208, 8192], P('wide', 'nar'), may hold values from 0.5 to 2
Outputs:
- mixed: bfloat16 [512, 8192], P('grp', ('nar', 'wide'))
The draws below stay inside these ranges and needn't reach their ends.
All inputs are finite; a program needn't handle non-finite values.
Results may differ from the reference program's by a relative error of at most 0.02.
Values may be sent and summed in bfloat16 or wider, within the bound.
No kernel may reach another device: no remote copies, remote signals or barrier semaphores. Data moves between devices by JAX's collectives and lax.ppermute only.
A program may use at most 128 MiB of HBM per device.

```python
import math
import jax
import jax.numpy as jnp
from jax import lax

D = 8192
FF = 26624
ROWS = 512
N_WIDE = 8
N_NAR = 4


def block_scale(key, shape, cuts, low, high):
    factor_of, own = 1.0, jax.random.fold_in(key, 6)
    for dim, shards_of in cuts:
        heights = jnp.exp(jax.random.uniform(jax.random.fold_in(own, dim), (shards_of,), jnp.float32, low / len(cuts), high / len(cuts)))
        factor_of = factor_of * jnp.repeat(heights, shape[dim] // shards_of).reshape([-1 if axis == dim else 1 for axis in range(len(shape))])
    return factor_of


def gaussian(stream_key, dims, width, reach, shards=(), kind=jnp.bfloat16):
    values = jax.random.normal(stream_key, dims, jnp.float32) * width
    if len(shards) > 0:
        values = block_scale(stream_key, dims, shards, -0.22, 0.18) * values
    return jnp.clip(values, min=-reach, max=reach).astype(kind)


def setup_inputs(seed: int = 0, part: int = 0) -> dict:
    splits = jax.random.split(jax.random.key(seed), 8)
    own_keys = jax.random.split(jax.random.fold_in(splits[7], part), 8)
    return {
        "tokens": gaussian(own_keys[0], (ROWS, D), 1.0, 6.0, ((1, 32),)),
        "gate_weight": gaussian(splits[1], (D, FF), D ** -0.5, 0.0625, ((0, 4), (1, 8))),
        "gate_scale": jnp.clip(jnp.exp(math.log(2.0) - 1.3862944 * jax.random.uniform(splits[2], (D // 128, FF), jnp.float32) ** block_scale(splits[2], (D // 128, FF), ((0, 4), (1, 8)), -0.2, 0.2)), 0.5, 2.0),
        "up_weight": gaussian(splits[3], (D, FF), D ** -0.5, 0.0625, ((0, 4), (1, 8))),
        "up_scale": jnp.clip(jnp.exp(math.log(2.0) - 1.3862944 * jax.random.uniform(splits[4], (D // 128, FF), jnp.float32) ** block_scale(splits[4], (D // 128, FF), ((0, 4), (1, 8)), -0.2, 0.2)), 0.5, 2.0),
        "down_weight": gaussian(splits[5], (FF, D), FF ** -0.5, 0.0390625, ((0, 8), (1, 4))),
        "down_scale": jnp.clip(jnp.exp(math.log(2.0) - 1.3862944 * jax.random.uniform(splits[6], (FF // 128, D), jnp.float32) ** block_scale(splits[6], (FF // 128, D), ((0, 8), (1, 4)), -0.2, 0.2)), 0.5, 2.0),
    }


def decode_weight(codes, scales):
    rows, cols = codes.shape
    blocks = codes.astype(jnp.float32).reshape(rows // 128, 128, cols) * scales[:, None, :]
    return blocks.reshape(rows, cols).astype(jnp.bfloat16)


def reference(tokens, gate_weight, gate_scale, up_weight, up_scale, down_weight, down_scale):
    row_count = tokens.shape[0]
    feat_block = D // N_NAR
    unit_block = FF // N_WIDE
    gate_deq = decode_weight(gate_weight, gate_scale)
    up_deq = decode_weight(up_weight, up_scale)
    down_deq = decode_weight(down_weight, down_scale)

    def first_section(running, block_index):
        offset = (block_index * feat_block).astype(jnp.int32)
        token_cols = lax.dynamic_slice_in_dim(tokens, offset, feat_block, 1)
        gate_rows = lax.dynamic_slice_in_dim(gate_deq, offset, feat_block, 0)
        up_rows = lax.dynamic_slice_in_dim(up_deq, offset, feat_block, 0)
        gate_part = jnp.dot(token_cols, gate_rows, preferred_element_type=jnp.float32).astype(jnp.bfloat16)
        up_part = jnp.dot(token_cols, up_rows, preferred_element_type=jnp.float32).astype(jnp.bfloat16)
        gate_part, up_part = lax.optimization_barrier((gate_part, up_part))
        return (running[0] + gate_part.astype(jnp.float32), running[1] + up_part.astype(jnp.float32)), None

    zero_pair = (jnp.zeros((row_count, FF), jnp.float32), jnp.zeros((row_count, FF), jnp.float32))
    (gate_sum, up_sum), _ = lax.scan(first_section, zero_pair, jnp.arange(N_NAR, dtype=jnp.int32))
    hidden = (jax.nn.silu(gate_sum) * up_sum).astype(jnp.bfloat16)

    def second_section(running, block_index):
        offset = (block_index * unit_block).astype(jnp.int32)
        hidden_cols = lax.dynamic_slice_in_dim(hidden, offset, unit_block, 1)
        down_rows = lax.dynamic_slice_in_dim(down_deq, offset, unit_block, 0)
        down_part = jnp.dot(hidden_cols, down_rows, preferred_element_type=jnp.float32).astype(jnp.bfloat16)
        down_part = lax.optimization_barrier(down_part)
        return running + down_part.astype(jnp.float32), None

    mixed_sum, _ = lax.scan(second_section, jnp.zeros((row_count, D), jnp.float32), jnp.arange(N_WIDE, dtype=jnp.int32))
    return mixed_sum.astype(jnp.bfloat16)
```

```python
import functools

import jax
import jax.numpy as jnp
from jax import lax
from jax.experimental import pallas as pl
from jax.experimental.pallas import tpu as pltpu
from jax.sharding import PartitionSpec as P

GROUP = 128
MIB = 1 << 20


def n_bits(size):
    return size.bit_length() - 1


def reverse_bits(value, bits):
    out = value * 0
    for b in range(bits):
        out = out + ((value >> b) & 1) * (1 << (bits - 1 - b))
    return out


def flip(array, axis, size, mask):
    return lax.ppermute(array, axis, [(i, i ^ mask) for i in range(size)])


def decode(codes, scales):
    rows, cols = codes.shape
    blocks = codes.reshape(rows // GROUP, GROUP, cols) * scales.astype(jnp.bfloat16)[:, None, :]
    return blocks.reshape(rows, cols)


def in_hbm(array):
    return pltpu.with_memory_space_constraint(array, pltpu.HBM)


def in_vmem(array):
    return pltpu.with_memory_space_constraint(array, pltpu.VMEM)


def after(array, *others):
    return lax.optimization_barrier((array, *others))[0]


def cost(size=1024):
    return pl.CostEstimate(flops=size, bytes_accessed=size, transcendentals=0)


def decode_kernel(first, block, w_ref, sc_ref, out_ref, arrived):
    size = out_ref.shape[0]

    def fetch(k):
        return pltpu.make_async_copy(
            w_ref.at[pl.ds(first + k * block, block)], out_ref.at[pl.ds(k * block, block)], arrived.at[k]
        )

    count = size // block
    for k in range(count):
        fetch(k).start()
    for k in range(count):
        fetch(k).wait()
        for g in range(k * block // GROUP, (k + 1) * block // GROUP):
            rows = slice(g * GROUP, (g + 1) * GROUP)
            out_ref[rows] = out_ref[rows] * sc_ref[first // GROUP + g : first // GROUP + g + 1].astype(jnp.bfloat16)


def decode_part(codes, scales, part, parts):
    depth, units = codes.shape
    size = depth // parts
    block = 256 if size % 256 == 0 else GROUP
    vmem = pl.BlockSpec(memory_space=pltpu.VMEM)
    return pl.pallas_call(
        functools.partial(decode_kernel, part * size, block),
        in_specs=[pl.BlockSpec(memory_space=pl.ANY), vmem],
        out_specs=vmem,
        out_shape=pltpu.VMEM((size, units), jnp.bfloat16),
        scratch_shapes=[pltpu.SemaphoreType.DMA((size // block,))],
        compiler_params=pltpu.CompilerParams(vmem_limit_bytes=6 * MIB),
        cost_estimate=cost(),
        name="decode",
    )(in_hbm(codes), scales)


def gate_up_kernel(n_tok, n_gate, n_up, place_ref, *refs):
    cuts = (n_tok, n_tok + n_gate, n_tok + n_gate + n_up)
    tok_refs, gate_refs, up_refs = refs[: cuts[0]], refs[cuts[0] : cuts[1]], refs[cuts[1] : cuts[2]]
    keep_ref, send_ref, x_ref = refs[cuts[2] :]
    shards = [ref.at[i] for ref in tok_refs for i in range(ref.shape[0])]
    bits = n_bits(len(shards))
    for p, shard in enumerate(shards):
        width = shard.shape[1]
        spot = pl.multiple_of((place_ref[0] ^ reverse_bits(p, bits)) * width, width)
        x_ref[:, pl.ds(spot, width)] = shard[...]
    half, quarter = keep_ref.shape[0], keep_ref.shape[2]
    units = gate_refs[0].shape[1]
    tile = 256 if units % 256 == 0 else 128

    def column(j, carry):
        cols = pl.ds(pl.multiple_of(j * tile, tile), tile)
        for s, w_refs in enumerate((gate_refs, up_refs)):
            part = sum(
                jnp.dot(
                    x_ref[:, k * w_ref.shape[0] : (k + 1) * w_ref.shape[0]],
                    w_ref[:, cols],
                    preferred_element_type=jnp.float32,
                )
                for k, w_ref in enumerate(w_refs)
            ).astype(jnp.bfloat16)
            for b in range(half):
                keep_ref[b, s, :, cols] = part[b * quarter : (b + 1) * quarter]
                send_ref[b, s, :, cols] = part[(half + b) * quarter : (half + b + 1) * quarter]
        return carry

    lax.fori_loop(0, units // tile, column, 0)


def gate_up(place, shards, gate, up, n_nar):
    count, (rows, width) = sum(t.shape[0] for t in shards), shards[0].shape[1:]
    depth, units = sum(g.shape[0] for g in gate), gate[0].shape[1]
    quarter = rows // n_nar
    shape = (n_nar // 2, 2, quarter, units)
    if width % 128:
        order = reverse_bits(place ^ jnp.arange(count), n_bits(count))
        x = jnp.take(jnp.concatenate(shards), order, axis=0).transpose(1, 0, 2).reshape(rows, depth)
        both = [
            jnp.dot(x, jnp.concatenate(w), preferred_element_type=jnp.float32)
            .astype(jnp.bfloat16)
            .reshape(2, n_nar // 2, quarter, units)
            for w in (gate, up)
        ]
        both = jnp.stack(both, axis=2)
        return both[0], both[1]
    out = jax.ShapeDtypeStruct(shape, jnp.bfloat16)
    vmem = pl.BlockSpec(memory_space=pltpu.VMEM)
    return pl.pallas_call(
        functools.partial(gate_up_kernel, len(shards), len(gate), len(up)),
        in_specs=[pl.BlockSpec(memory_space=pltpu.SMEM)] + [vmem] * (len(shards) + len(gate) + len(up)),
        out_specs=[vmem, vmem],
        scratch_shapes=[pltpu.VMEM((rows, depth), jnp.bfloat16)],
        out_shape=[out, out],
        compiler_params=pltpu.CompilerParams(vmem_limit_bytes=6 * MIB),
        cost_estimate=cost(),
        name="gate_up",
    )(place.reshape(1), *shards, *[in_vmem(w) for w in (*gate, *up)])


def down_kernel(parts, pieces, place_ref, *refs):
    h_refs, w_refs, (keep_ref, send_ref, h_ref) = refs[:parts], refs[parts : parts + pieces], refs[parts + pieces :]
    top = 0
    for ref in h_refs:
        h_ref[top : top + ref.shape[0]] = ref[...]
        top += ref.shape[0]
    half, _, width = keep_ref.shape
    bits = n_bits(2 * half)
    size = w_refs[0].shape[0]
    for out_ref, first in ((send_ref, half), (keep_ref, 0)):

        def block(i, carry, out_ref=out_ref, first=first):
            spot = pl.multiple_of((place_ref[0] ^ reverse_bits(first + i, bits)) * width, width)
            part = sum(
                jnp.dot(
                    h_ref[:, k * size : (k + 1) * size], w_ref[:, pl.ds(spot, width)], preferred_element_type=jnp.float32
                )
                for k, w_ref in enumerate(w_refs)
            )
            out_ref[i] = part.astype(jnp.bfloat16)
            return carry

        lax.fori_loop(0, half, block, 0)


def down(place, hidden, weights, n_wide):
    rows = sum(h.shape[0] for h in hidden)
    units, features = sum(w.shape[0] for w in weights), weights[0].shape[1]
    width, bits, half = features // n_wide, n_bits(n_wide), n_wide // 2
    if width % 128:
        part = jnp.dot(jnp.concatenate(hidden), jnp.concatenate(weights), preferred_element_type=jnp.float32)
        part = part.astype(jnp.bfloat16).reshape(rows, n_wide, width).transpose(1, 0, 2)
        part = jnp.take(part, place ^ reverse_bits(jnp.arange(n_wide), bits), axis=0)
        return part[:half], part[half:]
    out = jax.ShapeDtypeStruct((half, rows, width), jnp.bfloat16)
    vmem = pl.BlockSpec(memory_space=pltpu.VMEM)
    return pl.pallas_call(
        functools.partial(down_kernel, len(hidden), len(weights)),
        in_specs=[pl.BlockSpec(memory_space=pltpu.SMEM)] + [vmem] * (len(hidden) + len(weights)),
        out_specs=[vmem, vmem],
        scratch_shapes=[pltpu.VMEM((rows, units), jnp.bfloat16)],
        out_shape=[out, out],
        compiler_params=pltpu.CompilerParams(vmem_limit_bytes=6 * MIB),
        cost_estimate=cost(),
        name="down",
    )(place.reshape(1), *hidden, *[in_vmem(w) for w in weights])


def add(a, b):
    return (a.astype(jnp.float32) + b.astype(jnp.float32)).astype(jnp.bfloat16)


def kernel_call(kernel, shapes, *operands, name, size=1024):
    vmem = pl.BlockSpec(memory_space=pltpu.VMEM)
    return pl.pallas_call(
        kernel,
        in_specs=[vmem] * len(operands),
        out_specs=[vmem] * len(shapes),
        out_shape=[jax.ShapeDtypeStruct(shape, jnp.bfloat16) for shape in shapes],
        compiler_params=pltpu.CompilerParams(vmem_limit_bytes=4 * MIB),
        cost_estimate=cost(size),
        name=name,
    )(*operands)


def tiles_of(width):
    return 256 if width % 256 == 0 else 128 if width % 128 == 0 else width


def add_halves_kernel(a_ref, *refs):
    piece_refs, (first_ref, second_ref) = refs[:-2], refs[-2:]
    half, width = first_ref.shape[0], a_ref.shape[-1]
    tile = tiles_of(width)

    def columns(j, carry):
        cols = pl.ds(pl.multiple_of(j * tile, tile), tile)
        for i in range(2 * half):
            for s in (0, 1):
                total = add(a_ref[i, s, :, cols], piece_refs[2 * i + s][:, cols])
                (first_ref if i < half else second_ref)[i % half, s, :, cols] = total
        return carry

    lax.fori_loop(0, width // tile, columns, 0)


def add_halves(a, pieces):
    if a.shape[-1] % 128 or a.shape[-2] % 16:
        total = add(a, jnp.stack(pieces).reshape(a.shape))
        return total[: a.shape[0] // 2], total[a.shape[0] // 2 :]
    shape = (a.shape[0] // 2, *a.shape[1:])
    return kernel_call(add_halves_kernel, [shape, shape], a, *pieces, name="add_halves")


def gated_kernel(a_ref, b_ref, out_ref):
    width = out_ref.shape[-1]
    tile = tiles_of(width)

    def columns(j, carry):
        cols = pl.ds(pl.multiple_of(j * tile, tile), tile)
        gate, up = (a_ref[0, s, :, cols].astype(jnp.float32) + b_ref[0, s, :, cols].astype(jnp.float32) for s in (0, 1))
        out_ref[:, cols] = (gate / (1 + jnp.exp(-gate)) * up).astype(jnp.bfloat16)
        return carry

    lax.fori_loop(0, width // tile, columns, 0)


def gated_sum(a, b):
    if a.shape[-1] % 128 or a.shape[-2] % 16:
        gate, up = (a[0, s].astype(jnp.float32) + b[0, s].astype(jnp.float32) for s in (0, 1))
        return (jax.nn.silu(gate) * up).astype(jnp.bfloat16)
    return kernel_call(gated_kernel, [a.shape[2:]], a, b, name="gated", size=4 * MIB)[0]


def deal_kernel(edges, place_ref, x_ref, *out_refs):
    count = x_ref.shape[0]
    for i in range(count):
        source = place_ref[0] ^ reverse_bits(i, n_bits(count))
        for out_ref, lo, hi in zip(out_refs, edges, edges[1:]):
            out_ref[i] = x_ref[source, lo:hi]


def deal(place, x, edges):
    count, _, width = x.shape
    sizes = [hi - lo for lo, hi in zip(edges, edges[1:])]
    if width % 128 or any(size % 16 for size in sizes):
        x = jnp.take(x, place ^ reverse_bits(jnp.arange(count), n_bits(count)), axis=0)
        return [x[:, lo:hi] for lo, hi in zip(edges, edges[1:])]
    vmem = pl.BlockSpec(memory_space=pltpu.VMEM)
    return pl.pallas_call(
        functools.partial(deal_kernel, edges),
        in_specs=[pl.BlockSpec(memory_space=pltpu.SMEM), vmem],
        out_specs=[vmem] * len(sizes),
        out_shape=[jax.ShapeDtypeStruct((count, size, width), x.dtype) for size in sizes],
        compiler_params=pltpu.CompilerParams(vmem_limit_bytes=4 * MIB),
        cost_estimate=cost(),
        name="deal",
    )(place.reshape(1), x)


def collect_kernel(edges, place_ref, *refs):
    part_refs, out_ref = refs[:-1], refs[-1]
    count = out_ref.shape[0]
    for i in range(count):
        target = place_ref[0] ^ reverse_bits(i, n_bits(count))
        for part_ref, lo, hi in zip(part_refs, edges, edges[1:]):
            out_ref[target, lo:hi] = part_ref[i]


def collect(place, parts, edges):
    count, _, width = parts[0].shape
    if width % 128 or any((hi - lo) % 16 for lo, hi in zip(edges, edges[1:])):
        order = reverse_bits(place ^ jnp.arange(count), n_bits(count))
        return jnp.take(jnp.concatenate(parts, axis=1), order, axis=0)
    vmem = pl.BlockSpec(memory_space=pltpu.VMEM)
    return pl.pallas_call(
        functools.partial(collect_kernel, edges),
        in_specs=[pl.BlockSpec(memory_space=pltpu.SMEM)] + [vmem] * len(parts),
        out_specs=vmem,
        out_shape=jax.ShapeDtypeStruct((count, edges[-1], width), parts[0].dtype),
        compiler_params=pltpu.CompilerParams(vmem_limit_bytes=4 * MIB),
        cost_estimate=cost(),
        name="collect",
    )(place.reshape(1), *parts)


def on_device(n_wide, n_nar, cuts, tokens, gw, gs, uw, us, dw, ds):
    wide, nar = lax.axis_index("wide"), lax.axis_index("nar")
    nar_bits, wide_bits = n_bits(n_nar), n_bits(n_wide)
    rows, width = tokens.shape
    fast = width % 128 == 0
    n = len(cuts)
    edges = [sum(cuts[:k]) // n_nar for k in range(n + 1)]
    dealt = deal(nar, after(tokens.reshape(n_nar, rows // n_nar, width), wide), edges)
    tok = [[t.reshape(1, -1, width)] for t in dealt]
    level = [wide_bits] * n

    def gather_tokens(k, to, *others):
        while level[k] > to:
            level[k] -= 1
            got = flip(tok[k][0], "wide", n_wide, 1 << level[k])
            if others:
                got = after(got, *others)
            tok[k] = [jnp.concatenate([tok[k][0], got])] if level[k] else [tok[k][0], got]

    def sum_core(k, *others):
        for b in range(nar_bits - 1):
            got = [flip(send[k][i, j], "nar", n_nar, 1 << b) for i in range(send[k].shape[0]) for j in (0, 1)]
            if others:
                got[0] = after(got[0], *others)
            keep[k], send[k] = add_halves(keep[k], got)

    far = 1 << (nar_bits - 1)

    def gated(k, *others):
        got = after(flip(send[k], "nar", n_nar, far), *others)
        hidden[k] = [gated_sum(keep[k], got)]
        hidden[k].append(flip(hidden[k][0], "nar", n_nar, far))

    def gather_hidden(k):
        for b in reversed(range(nar_bits - 1)):
            hidden[k] = hidden[k] + [flip(g, "nar", n_nar, 1 << b) for g in hidden[k]]

    keep, send, hidden = [None] * n, [None] * n, [None] * n
    parts, todo = [None] * n, [0] * n

    def scatter(k, to):
        while todo[k] > to:
            total = add(parts[k][0], flip(parts[k][1], "wide", n_wide, 1 << (wide_bits - todo[k])))
            todo[k] -= 1
            half = total.shape[0] // 2
            parts[k] = (total[:half], total[half:]) if todo[k] else (total,)

    def products(k, *others):
        keep[k], send[k] = gate_up(wide, [after(tok[k][0], *others), *tok[k][1:]], gate, up, n_nar)

    def finish(k, weights, *others):
        hidden[k][0] = after(hidden[k][0], *others)
        parts[k], todo[k] = down(wide, hidden[k], weights, n_wide), wide_bits

    if not fast or n != 4 or wide_bits < 2:
        gate, up, down_w = [decode(gw, gs)], [decode(uw, us)], [decode(dw, ds)]
        for k in range(n):
            gather_tokens(k, 0)
            products(k)
            sum_core(k)
            gated(k)
            gather_hidden(k)
            finish(k, down_w)
            scatter(k, 0)
    else:
        gate = [decode_part(after(gw, dealt[0]), gs, 0, 2)]
        for k in range(4):
            gather_tokens(k, wide_bits - 1, gate[0])
        gate.append(decode_part(after(gw, gate[0], tok[0][0]), gs, 1, 2))
        for k in (0, 1):
            gather_tokens(k, 1, gate[1])
        up = [decode_part(after(uw, tok[0][0], tok[1][0]), us, 0, 1)]
        for k in (2, 3):
            gather_tokens(k, 1, up[0])
        gather_tokens(0, 0, up[0])
        products(0)
        gather_tokens(1, 0, send[0])
        send[0] = after(send[0], tok[1][1], tok[2][0], tok[3][0])
        gather_tokens(2, 0)
        gather_tokens(3, 0)
        sum_core(0)
        down_w = []
        for k in range(3):
            products(k + 1, send[k], *(hidden[k - 1][:2] if k > 0 else []))
            if k < 2:
                down_w.append(decode_part(after(dw, send[k + 1]), ds, k, 2))
                tok[k + 2][1] = after(tok[k + 2][1], send[k + 1])
                send[k + 1] = after(send[k + 1], tok[k + 2][1], down_w[k])
            else:
                finish(0, down_w, send[3])
                send[3] = after(send[3], parts[0][1])
            gated(k, send[k + 1])
            sum_core(k + 1, hidden[k][0])
            gather_hidden(k)
        scatter(0, wide_bits - 1)
        finish(1, down_w, send[3], *parts[0])
        scatter(0, wide_bits - 2)
        scatter(1, wide_bits - 1)
        finish(2, down_w, *parts[0], *parts[1])
        gated(3, parts[2][1])
        scatter(0, max(wide_bits - 3, 0))
        scatter(1, wide_bits - 2)
        scatter(2, wide_bits - 1)
        gather_hidden(3)
        finish(3, down_w, *parts[0], *parts[1], *parts[2])
        for k in range(4):
            scatter(k, 0)
    outs = [part[0].reshape(n_nar, -1, width) for part in parts]
    return collect(nar, outs, edges).reshape(rows, width)


def solution(mesh):
    n_wide, n_nar = mesh.shape["wide"], mesh.shape["nar"]

    def local(tokens, *weights):
        rows = tokens.shape[0]
        cuts = (128,) * (rows // 128) if 128 // n_nar >= 16 else (rows,)
        return on_device(n_wide, n_nar, cuts, tokens, *weights)

    in_specs = (
        P("grp", ("nar", "wide")),
        P("nar", "wide"),
        P("nar", "wide"),
        P("nar", "wide"),
        P("nar", "wide"),
        P("wide", "nar"),
        P("wide", "nar"),
    )
    return jax.shard_map(
        local, mesh=mesh, in_specs=in_specs, out_specs=P("grp", ("nar", "wide")), check_vma=False
    )
```

```python
import functools

import jax
import jax.numpy as jnp
from jax import lax
from jax.experimental import pallas as pl
from jax.experimental.pallas import tpu as pltpu
from jax.sharding import PartitionSpec as P

GROUP = 128
MIB = 1 << 20


def n_bits(size):
    return size.bit_length() - 1


def reverse_bits(value, bits):
    out = value * 0
    for b in range(bits):
        out = out + ((value >> b) & 1) * (1 << (bits - 1 - b))
    return out


def spread(value, order):
    return sum(((value >> (len(order) - 1 - s)) & 1) << b for s, b in enumerate(order))


def flip(array, axis, size, mask):
    return lax.ppermute(array, axis, [(i, i ^ mask) for i in range(size)])


def decode(codes, scales):
    rows, cols = codes.shape
    blocks = codes.reshape(rows // GROUP, GROUP, cols) * scales.astype(jnp.bfloat16)[:, None, :]
    return blocks.reshape(rows, cols)


def in_hbm(array):
    return pltpu.with_memory_space_constraint(array, pltpu.HBM)


def in_vmem(array):
    return pltpu.with_memory_space_constraint(array, pltpu.VMEM)


def after(array, *others):
    return lax.optimization_barrier((array, *others))[0]


def cost(size=1024):
    return pl.CostEstimate(flops=size, bytes_accessed=size, transcendentals=0)


def decode_kernel(first, block, w_ref, sc_ref, out_ref, arrived):
    size = out_ref.shape[0]

    def fetch(k):
        return pltpu.make_async_copy(
            w_ref.at[pl.ds(first + k * block, block)], out_ref.at[pl.ds(k * block, block)], arrived.at[k]
        )

    count = size // block
    for k in range(count):
        fetch(k).start()
    for k in range(count):
        fetch(k).wait()
        for g in range(k * block // GROUP, (k + 1) * block // GROUP):
            rows = slice(g * GROUP, (g + 1) * GROUP)
            out_ref[rows] = out_ref[rows] * sc_ref[first // GROUP + g : first // GROUP + g + 1].astype(jnp.bfloat16)


def decode_part(codes, scales, part, parts):
    depth, units = codes.shape
    size = depth // parts
    block = 256 if size % 256 == 0 else GROUP
    vmem = pl.BlockSpec(memory_space=pltpu.VMEM)
    return pl.pallas_call(
        functools.partial(decode_kernel, part * size, block),
        in_specs=[pl.BlockSpec(memory_space=pl.ANY), vmem],
        out_specs=vmem,
        out_shape=pltpu.VMEM((size, units), jnp.bfloat16),
        scratch_shapes=[pltpu.SemaphoreType.DMA((size // block,))],
        compiler_params=pltpu.CompilerParams(vmem_limit_bytes=6 * MIB),
        cost_estimate=cost(),
        name="decode",
    )(in_hbm(codes), scales)


def gate_up_kernel(n_tok, n_gate, n_up, place_ref, *refs):
    cuts = (n_tok, n_tok + n_gate, n_tok + n_gate + n_up)
    tok_refs, gate_refs, up_refs = refs[: cuts[0]], refs[cuts[0] : cuts[1]], refs[cuts[1] : cuts[2]]
    keep_ref, send_ref, x_ref = refs[cuts[2] :]
    shards = [ref.at[i] for ref in tok_refs for i in range(ref.shape[0])]
    bits = n_bits(len(shards))
    for p, shard in enumerate(shards):
        width = shard.shape[1]
        spot = pl.multiple_of((place_ref[0] ^ reverse_bits(p, bits)) * width, width)
        x_ref[:, pl.ds(spot, width)] = shard[...]
    half, quarter = keep_ref.shape[0], keep_ref.shape[2]
    units = gate_refs[0].shape[1]
    tile = 256 if units % 256 == 0 else 128

    def column(j, carry):
        cols = pl.ds(pl.multiple_of(j * tile, tile), tile)
        for s, w_refs in enumerate((gate_refs, up_refs)):
            part = sum(
                jnp.dot(
                    x_ref[:, k * w_ref.shape[0] : (k + 1) * w_ref.shape[0]],
                    w_ref[:, cols],
                    preferred_element_type=jnp.float32,
                )
                for k, w_ref in enumerate(w_refs)
            ).astype(jnp.bfloat16)
            for b in range(half):
                keep_ref[b, s, :, cols] = part[b * quarter : (b + 1) * quarter]
                send_ref[b, s, :, cols] = part[(half + b) * quarter : (half + b + 1) * quarter]
        return carry

    lax.fori_loop(0, units // tile, column, 0)


def gate_up(place, shards, gate, up, n_nar):
    count, (rows, width) = sum(t.shape[0] for t in shards), shards[0].shape[1:]
    depth, units = sum(g.shape[0] for g in gate), gate[0].shape[1]
    quarter = rows // n_nar
    shape = (n_nar // 2, 2, quarter, units)
    if width % 128:
        order = reverse_bits(place ^ jnp.arange(count), n_bits(count))
        x = jnp.take(jnp.concatenate(shards), order, axis=0).transpose(1, 0, 2).reshape(rows, depth)
        both = [
            jnp.dot(x, jnp.concatenate(w), preferred_element_type=jnp.float32)
            .astype(jnp.bfloat16)
            .reshape(2, n_nar // 2, quarter, units)
            for w in (gate, up)
        ]
        both = jnp.stack(both, axis=2)
        return both[0], both[1]
    out = jax.ShapeDtypeStruct(shape, jnp.bfloat16)
    vmem = pl.BlockSpec(memory_space=pltpu.VMEM)
    return pl.pallas_call(
        functools.partial(gate_up_kernel, len(shards), len(gate), len(up)),
        in_specs=[pl.BlockSpec(memory_space=pltpu.SMEM)] + [vmem] * (len(shards) + len(gate) + len(up)),
        out_specs=[vmem, vmem],
        scratch_shapes=[pltpu.VMEM((rows, depth), jnp.bfloat16)],
        out_shape=[out, out],
        compiler_params=pltpu.CompilerParams(vmem_limit_bytes=6 * MIB),
        cost_estimate=cost(),
        name="gate_up",
    )(place.reshape(1), *shards, *[in_vmem(w) for w in (*gate, *up)])


def down_kernel(parts, pieces, order, place_ref, *refs):
    h_refs, w_refs, (keep_ref, send_ref, h_ref) = refs[:parts], refs[parts : parts + pieces], refs[parts + pieces :]
    top = 0
    for ref in h_refs:
        h_ref[top : top + ref.shape[0]] = ref[...]
        top += ref.shape[0]
    half, _, width = keep_ref.shape
    size = w_refs[0].shape[0]
    for out_ref, first in ((send_ref, half), (keep_ref, 0)):

        def block(i, carry, out_ref=out_ref, first=first):
            spot = pl.multiple_of((place_ref[0] ^ spread(first + i, order)) * width, width)
            part = sum(
                jnp.dot(
                    h_ref[:, k * size : (k + 1) * size], w_ref[:, pl.ds(spot, width)], preferred_element_type=jnp.float32
                )
                for k, w_ref in enumerate(w_refs)
            )
            out_ref[i] = part.astype(jnp.bfloat16)
            return carry

        lax.fori_loop(0, half, block, 0)


def down(place, hidden, weights, n_wide, order):
    rows = sum(h.shape[0] for h in hidden)
    units, features = sum(w.shape[0] for w in weights), weights[0].shape[1]
    width, half = features // n_wide, n_wide // 2
    if width % 128:
        part = jnp.dot(jnp.concatenate(hidden), jnp.concatenate(weights), preferred_element_type=jnp.float32)
        part = part.astype(jnp.bfloat16).reshape(rows, n_wide, width).transpose(1, 0, 2)
        part = jnp.take(part, place ^ spread(jnp.arange(n_wide), order), axis=0)
        return part[:half], part[half:]
    out = jax.ShapeDtypeStruct((half, rows, width), jnp.bfloat16)
    vmem = pl.BlockSpec(memory_space=pltpu.VMEM)
    return pl.pallas_call(
        functools.partial(down_kernel, len(hidden), len(weights), order),
        in_specs=[pl.BlockSpec(memory_space=pltpu.SMEM)] + [vmem] * (len(hidden) + len(weights)),
        out_specs=[vmem, vmem],
        scratch_shapes=[pltpu.VMEM((rows, units), jnp.bfloat16)],
        out_shape=[out, out],
        compiler_params=pltpu.CompilerParams(vmem_limit_bytes=6 * MIB),
        cost_estimate=cost(),
        name="down",
    )(place.reshape(1), *hidden, *[in_vmem(w) for w in weights])


def add(a, b):
    return (a.astype(jnp.float32) + b.astype(jnp.float32)).astype(jnp.bfloat16)


def kernel_call(kernel, shapes, *operands, name, size=1024):
    vmem = pl.BlockSpec(memory_space=pltpu.VMEM)
    return pl.pallas_call(
        kernel,
        in_specs=[vmem] * len(operands),
        out_specs=[vmem] * len(shapes),
        out_shape=[jax.ShapeDtypeStruct(shape, jnp.bfloat16) for shape in shapes],
        compiler_params=pltpu.CompilerParams(vmem_limit_bytes=4 * MIB),
        cost_estimate=cost(size),
        name=name,
    )(*operands)


def tiles_of(width):
    return 256 if width % 256 == 0 else 128 if width % 128 == 0 else width


def add_halves_kernel(a_ref, *refs):
    piece_refs, (first_ref, second_ref) = refs[:-2], refs[-2:]
    half, rows, width = first_ref.shape[0], a_ref.shape[-2], a_ref.shape[-1]
    tile = tiles_of(width)

    def columns(j, carry):
        cols = pl.ds(pl.multiple_of(j * tile, tile), tile)
        top = 0
        for ref in piece_refs:
            size = ref.shape[0]
            i, s, row = top // (2 * rows), top // rows % 2, top % rows
            total = add(a_ref[i, s, row : row + size, cols], ref[:, cols])
            (first_ref if i < half else second_ref)[i % half, s, row : row + size, cols] = total
            top += size
        return carry

    lax.fori_loop(0, width // tile, columns, 0)


def add_halves(a, pieces):
    if a.shape[-1] % 128 or a.shape[-2] % 16:
        total = add(a, jnp.stack(pieces).reshape(a.shape))
        return total[: a.shape[0] // 2], total[a.shape[0] // 2 :]
    shape = (a.shape[0] // 2, *a.shape[1:])
    return kernel_call(add_halves_kernel, [shape, shape], a, *pieces, name="add_halves")


def gated_kernel(a_ref, b_ref, out_ref):
    width = out_ref.shape[-1]
    tile = tiles_of(width)

    def columns(j, carry):
        cols = pl.ds(pl.multiple_of(j * tile, tile), tile)
        gate, up = (a_ref[0, s, :, cols].astype(jnp.float32) + b_ref[0, s, :, cols].astype(jnp.float32) for s in (0, 1))
        out_ref[:, cols] = (gate / (1 + jnp.exp(-gate)) * up).astype(jnp.bfloat16)
        return carry

    lax.fori_loop(0, width // tile, columns, 0)


def gated_sum(a, b):
    if a.shape[-1] % 128 or a.shape[-2] % 16:
        gate, up = (a[0, s].astype(jnp.float32) + b[0, s].astype(jnp.float32) for s in (0, 1))
        return (jax.nn.silu(gate) * up).astype(jnp.bfloat16)
    return kernel_call(gated_kernel, [a.shape[2:]], a, b, name="gated", size=8 * MIB)[0]


def deal_kernel(edges, place_ref, x_ref, *out_refs):
    count = x_ref.shape[0]
    for i in range(count):
        source = place_ref[0] ^ reverse_bits(i, n_bits(count))
        for out_ref, lo, hi in zip(out_refs, edges, edges[1:]):
            out_ref[i] = x_ref[source, lo:hi]


def deal(place, x, edges):
    count, _, width = x.shape
    sizes = [hi - lo for lo, hi in zip(edges, edges[1:])]
    if width % 128 or any(size % 16 for size in sizes):
        x = jnp.take(x, place ^ reverse_bits(jnp.arange(count), n_bits(count)), axis=0)
        return [x[:, lo:hi] for lo, hi in zip(edges, edges[1:])]
    vmem = pl.BlockSpec(memory_space=pltpu.VMEM)
    return pl.pallas_call(
        functools.partial(deal_kernel, edges),
        in_specs=[pl.BlockSpec(memory_space=pltpu.SMEM), vmem],
        out_specs=[vmem] * len(sizes),
        out_shape=[jax.ShapeDtypeStruct((count, size, width), x.dtype) for size in sizes],
        compiler_params=pltpu.CompilerParams(vmem_limit_bytes=4 * MIB),
        cost_estimate=cost(),
        name="deal",
    )(place.reshape(1), x)


def collect_kernel(edges, place_ref, *refs):
    part_refs, out_ref = refs[:-1], refs[-1]
    count = out_ref.shape[0]
    pieces = [ref.at[m] for ref in part_refs for m in range(ref.shape[0])]
    for i in range(count):
        target = place_ref[0] ^ reverse_bits(i, n_bits(count))
        for piece, lo, hi in zip(pieces, edges, edges[1:]):
            out_ref[target, lo:hi] = piece[i]


def collect(place, parts, edges):
    _, count, _, width = parts[0].shape
    if width % 128 or any((hi - lo) % 16 for lo, hi in zip(edges, edges[1:])):
        order = reverse_bits(place ^ jnp.arange(count), n_bits(count))
        return jnp.take(jnp.concatenate([piece for part in parts for piece in part], axis=1), order, axis=0)
    vmem = pl.BlockSpec(memory_space=pltpu.VMEM)
    return pl.pallas_call(
        functools.partial(collect_kernel, edges),
        in_specs=[pl.BlockSpec(memory_space=pltpu.SMEM)] + [vmem] * len(parts),
        out_specs=vmem,
        out_shape=jax.ShapeDtypeStruct((count, edges[-1], width), parts[0].dtype),
        compiler_params=pltpu.CompilerParams(vmem_limit_bytes=4 * MIB),
        cost_estimate=cost(),
        name="collect",
    )(place.reshape(1), *parts)


def on_device(n_wide, n_nar, cuts, tokens, gw, gs, uw, us, dw, ds):
    wide, nar = lax.axis_index("wide"), lax.axis_index("nar")
    nar_bits, wide_bits = n_bits(n_nar), n_bits(n_wide)
    rows, width = tokens.shape
    fast = width % 128 == 0
    n = len(cuts)
    edges = [sum(cuts[:k]) // n_nar for k in range(n + 1)]
    dealt = deal(nar, after(tokens.reshape(n_nar, rows // n_nar, width), wide), edges)
    tok = [[t.reshape(1, -1, width)] for t in dealt]
    level = [wide_bits] * n

    def gather_tokens(k, to, *others):
        while level[k] > to:
            level[k] -= 1
            got = flip(tok[k][0], "wide", n_wide, 1 << level[k])
            if others:
                got = after(got, *others)
            tok[k] = [jnp.concatenate([tok[k][0], got])] if level[k] else [tok[k][0], got]

    def sum_core(k, pieces=8):
        for b in range(nar_bits - 1):
            flat = send[k].reshape(-1, send[k].shape[-1])
            size = min(max(flat.shape[0] // pieces, 16), send[k].shape[-2])
            got = [flip(flat[i : i + size], "nar", n_nar, 1 << b) for i in range(0, flat.shape[0], size)]
            keep[k], send[k] = add_halves(keep[k], got)

    far = 1 << (nar_bits - 1)

    def gated(k, *others):
        got = after(flip(send[k], "nar", n_nar, far), *others)
        hidden[k] = [gated_sum(keep[k], got)]
        hidden[k].append(flip(hidden[k][0], "nar", n_nar, far))

    def gather_hidden(k, pieces=1):
        for b in reversed(range(nar_bits - 1)):
            cut = [piece for g in hidden[k] for piece in jnp.split(g, pieces)]
            hidden[k] = hidden[k] + [flip(g, "nar", n_nar, 1 << b) for g in cut]

    keep, send, hidden = [None] * n, [None] * n, [None] * n
    parts, todo = [None] * n, [0] * n
    orders = [tuple(range(wide_bits)) if k != 2 or wide_bits < 2 else (1, 0, *range(2, wide_bits)) for k in range(n)]

    def scatter(k, to, *others, split=False):
        while todo[k] > to:
            mask = 1 << orders[k][wide_bits - todo[k]]
            todo[k] -= 1
            mine, other = parts[k]
            half = mine.shape[0] // 2
            if todo[k] and split:
                got = [flip(other[:half], "wide", n_wide, mask), flip(other[half:], "wide", n_wide, mask)]
                got = [after(g, *others) if others else g for g in got]
                parts[k] = (add(mine[:half], got[0]), add(mine[half:], got[1]))
            else:
                got = flip(other, "wide", n_wide, mask)
                total = add(mine, after(got, *others) if others else got)
                parts[k] = (total[:half], total[half:]) if todo[k] else (total,)

    def products(k, *others):
        keep[k], send[k] = gate_up(wide, [after(tok[k][0], *others), *tok[k][1:]], gate, up, n_nar)

    def finish(k, weights, *others):
        chunks = k if isinstance(k, list) else [k]
        rows_of = [g for j in chunks for g in hidden[j]]
        rows_of[0] = after(rows_of[0], *others)
        k = chunks[0]
        parts[k], todo[k] = down(wide, rows_of, weights, n_wide, orders[k]), wide_bits

    if not fast or n != 4 or wide_bits < 2:
        gate, up, down_w = [decode(gw, gs)], [decode(uw, us)], [decode(dw, ds)]
        for k in range(n):
            gather_tokens(k, 0)
            products(k)
            sum_core(k)
            gated(k)
            gather_hidden(k)
            finish(k, down_w)
            scatter(k, 0)
    else:
        gate = [decode_part(after(gw, dealt[0]), gs, 0, 2)]
        for k in (0, 1):
            gather_tokens(k, wide_bits - 1, gate[0])
        gate.append(decode_part(after(gw, gate[0], tok[0][0]), gs, 1, 2))
        for k in (2, 3):
            gather_tokens(k, wide_bits - 1, gate[1])
        for k in (0, 1):
            gather_tokens(k, 1, gate[1])
        up = [decode_part(after(uw, tok[0][0], tok[1][0]), us, 0, 1)]
        for k in (2, 3):
            gather_tokens(k, 1, up[0])
        gather_tokens(0, 0, up[0])
        products(0)
        gather_tokens(1, 0, send[0])
        send[0] = after(send[0], tok[1][1], tok[2][0], tok[3][0])
        tok[2], tok[3] = [after(tok[2][0], send[0])], [after(tok[3][0], send[0])]
        gather_tokens(2, 0)
        gather_tokens(3, 0)
        sum_core(0, 4)
        down_w = []
        for k in range(3):
            products(k + 1, send[0] if k == 0 else hidden[k - 1][0])
            if k < 2:
                tok[k + 2][1] = after(tok[k + 2][1], send[k + 1])
                send[k + 1] = after(send[k + 1], tok[k + 2][1])
            sum_core(k + 1)
            others = [send[k + 1]]
            if k > 0:
                down_w.append(decode_part(after(dw, send[k + 1]), ds, k - 1, 2))
                others += [down_w[-1], hidden[k - 1][1]]
            gated(k, *others)
        for j in (0, 1):
            hidden[j] = [after(g, hidden[2][0]) for g in hidden[j]]
            gather_hidden(j, 1)
        finish([0, 1], down_w, hidden[2][0])
        gated(3, parts[0][1])
        gather_hidden(2, 2)
        finish(2, down_w, hidden[3][0])
        scatter(0, wide_bits - 1, parts[2][1], split=True)
        gather_hidden(3, 1)
        finish(3, down_w, *parts[0])
        scatter(0, wide_bits - 2, parts[3][1])
        scatter(2, wide_bits - 1, parts[3][1])
        for k in (0, 2, 3):
            scatter(k, 0)
        parts = [parts[0], parts[2], parts[3]]
    outs = [part[0].reshape(-1, n_nar, cuts[0] // n_nar, width) for part in parts]
    return collect(nar, outs, edges).reshape(rows, width)


def solution(mesh):
    n_wide, n_nar = mesh.shape["wide"], mesh.shape["nar"]

    def local(tokens, *weights):
        rows = tokens.shape[0]
        cuts = (128,) * (rows // 128) if 128 // n_nar >= 16 else (rows,)
        return on_device(n_wide, n_nar, cuts, tokens, *weights)

    in_specs = (
        P("grp", ("nar", "wide")),
        P("nar", "wide"),
        P("nar", "wide"),
        P("nar", "wide"),
        P("nar", "wide"),
        P("wide", "nar"),
        P("wide", "nar"),
    )
    return jax.shard_map(
        local, mesh=mesh, in_specs=in_specs, out_specs=P("grp", ("nar", "wide")), check_vma=False
    )
```

```python
import functools

import jax
import jax.numpy as jnp
from jax import lax
from jax.experimental import pallas as pl
from jax.experimental.pallas import tpu as pltpu
from jax.sharding import PartitionSpec as P

GROUP = 128
MIB = 1 << 20


def n_bits(size):
    return size.bit_length() - 1


def reverse_bits(value, bits):
    out = value * 0
    for b in range(bits):
        out = out + ((value >> b) & 1) * (1 << (bits - 1 - b))
    return out


def spread(value, order):
    return sum(((value >> (len(order) - 1 - s)) & 1) << b for s, b in enumerate(order))


def flip(array, axis, size, mask):
    return lax.ppermute(array, axis, [(i, i ^ mask) for i in range(size)])


def decode(codes, scales):
    rows, cols = codes.shape
    blocks = codes.reshape(rows // GROUP, GROUP, cols) * scales.astype(jnp.bfloat16)[:, None, :]
    return blocks.reshape(rows, cols)


def in_hbm(array):
    return pltpu.with_memory_space_constraint(array, pltpu.HBM)


def in_vmem(array):
    return pltpu.with_memory_space_constraint(array, pltpu.VMEM)


def after(array, *others):
    return lax.optimization_barrier((array, *others))[0]


def cost(size=1024):
    return pl.CostEstimate(flops=size, bytes_accessed=size, transcendentals=0)


def decode_kernel(first, block, w_ref, sc_ref, out_ref, scale_ref, arrived, scaled):
    size = out_ref.shape[0]
    scales = pltpu.make_async_copy(sc_ref, scale_ref, scaled)

    def fetch(k):
        return pltpu.make_async_copy(
            w_ref.at[pl.ds(first + k * block, block)], out_ref.at[pl.ds(k * block, block)], arrived.at[k]
        )

    count = size // block
    scales.start()
    for k in range(count):
        fetch(k).start()
    scales.wait()
    for k in range(count):
        fetch(k).wait()
        for g in range(k * block // GROUP, (k + 1) * block // GROUP):
            rows = slice(g * GROUP, (g + 1) * GROUP)
            scale = scale_ref[first // GROUP + g : first // GROUP + g + 1]
            out_ref[rows] = out_ref[rows] * scale.astype(jnp.bfloat16)


def decode_part(codes, scales, part, parts):
    depth, units = codes.shape
    size = depth // parts
    block = 256 if size % 256 == 0 else GROUP
    hbm = pl.BlockSpec(memory_space=pl.ANY)
    return pl.pallas_call(
        functools.partial(decode_kernel, part * size, block),
        in_specs=[hbm, hbm],
        out_specs=pl.BlockSpec(memory_space=pltpu.VMEM),
        out_shape=pltpu.VMEM((size, units), jnp.bfloat16),
        scratch_shapes=[
            pltpu.VMEM(scales.shape, jnp.float32),
            pltpu.SemaphoreType.DMA((size // block,)),
            pltpu.SemaphoreType.DMA,
        ],
        compiler_params=pltpu.CompilerParams(vmem_limit_bytes=6 * MIB),
        cost_estimate=cost(),
        name="decode",
    )(in_hbm(codes), in_hbm(scales))


def gate_up_kernel(n_tok, n_gate, n_up, place_ref, *refs):
    cuts = (n_tok, n_tok + n_gate, n_tok + n_gate + n_up)
    tok_refs, gate_refs, up_refs = refs[: cuts[0]], refs[cuts[0] : cuts[1]], refs[cuts[1] : cuts[2]]
    keep_ref, send_ref, x_ref = refs[cuts[2] :]
    shards = [ref.at[i] for ref in tok_refs for i in range(ref.shape[0])]
    bits = n_bits(len(shards))
    for p, shard in enumerate(shards):
        width = shard.shape[1]
        spot = pl.multiple_of((place_ref[0] ^ reverse_bits(p, bits)) * width, width)
        x_ref[:, pl.ds(spot, width)] = shard[...]
    half, quarter = keep_ref.shape[0], keep_ref.shape[2]
    units = gate_refs[0].shape[1]
    tile = 256 if units % 256 == 0 else 128

    def column(j, carry):
        cols = pl.ds(pl.multiple_of(j * tile, tile), tile)
        for s, w_refs in enumerate((gate_refs, up_refs)):
            part = sum(
                jnp.dot(
                    x_ref[:, k * w_ref.shape[0] : (k + 1) * w_ref.shape[0]],
                    w_ref[:, cols],
                    preferred_element_type=jnp.float32,
                )
                for k, w_ref in enumerate(w_refs)
            ).astype(jnp.bfloat16)
            for b in range(half):
                keep_ref[b, s, :, cols] = part[b * quarter : (b + 1) * quarter]
                send_ref[b, s, :, cols] = part[(half + b) * quarter : (half + b + 1) * quarter]
        return carry

    lax.fori_loop(0, units // tile, column, 0)


def gate_up(place, shards, gate, up, n_nar):
    count, (rows, width) = sum(t.shape[0] for t in shards), shards[0].shape[1:]
    depth, units = sum(g.shape[0] for g in gate), gate[0].shape[1]
    quarter = rows // n_nar
    shape = (n_nar // 2, 2, quarter, units)
    if width % 128:
        order = reverse_bits(place ^ jnp.arange(count), n_bits(count))
        x = jnp.take(jnp.concatenate(shards), order, axis=0).transpose(1, 0, 2).reshape(rows, depth)
        both = [
            jnp.dot(x, jnp.concatenate(w), preferred_element_type=jnp.float32)
            .astype(jnp.bfloat16)
            .reshape(2, n_nar // 2, quarter, units)
            for w in (gate, up)
        ]
        both = jnp.stack(both, axis=2)
        return both[0], both[1]
    out = jax.ShapeDtypeStruct(shape, jnp.bfloat16)
    vmem = pl.BlockSpec(memory_space=pltpu.VMEM)
    return pl.pallas_call(
        functools.partial(gate_up_kernel, len(shards), len(gate), len(up)),
        in_specs=[pl.BlockSpec(memory_space=pltpu.SMEM)] + [vmem] * (len(shards) + len(gate) + len(up)),
        out_specs=[vmem, vmem],
        scratch_shapes=[pltpu.VMEM((rows, depth), jnp.bfloat16)],
        out_shape=[out, out],
        compiler_params=pltpu.CompilerParams(vmem_limit_bytes=6 * MIB),
        cost_estimate=cost(),
        name="gate_up",
    )(place.reshape(1), *shards, *[in_vmem(w) for w in (*gate, *up)])


def down_kernel(parts, pieces, order, place_ref, *refs):
    h_refs, w_refs, (keep_ref, send_ref, h_ref) = refs[:parts], refs[parts : parts + pieces], refs[parts + pieces :]
    top = 0
    for ref in h_refs:
        h_ref[top : top + ref.shape[0]] = ref[...]
        top += ref.shape[0]
    half, _, width = keep_ref.shape
    size = w_refs[0].shape[0]
    for out_ref, first in ((send_ref, half), (keep_ref, 0)):

        def block(i, carry, out_ref=out_ref, first=first):
            spot = pl.multiple_of((place_ref[0] ^ spread(first + i, order)) * width, width)
            part = sum(
                jnp.dot(
                    h_ref[:, k * size : (k + 1) * size], w_ref[:, pl.ds(spot, width)], preferred_element_type=jnp.float32
                )
                for k, w_ref in enumerate(w_refs)
            )
            out_ref[i] = part.astype(jnp.bfloat16)
            return carry

        lax.fori_loop(0, half, block, 0)


def down(place, hidden, weights, n_wide, order):
    rows = sum(h.shape[0] for h in hidden)
    units, features = sum(w.shape[0] for w in weights), weights[0].shape[1]
    width, half = features // n_wide, n_wide // 2
    if width % 128:
        part = jnp.dot(jnp.concatenate(hidden), jnp.concatenate(weights), preferred_element_type=jnp.float32)
        part = part.astype(jnp.bfloat16).reshape(rows, n_wide, width).transpose(1, 0, 2)
        part = jnp.take(part, place ^ spread(jnp.arange(n_wide), order), axis=0)
        return part[:half], part[half:]
    out = jax.ShapeDtypeStruct((half, rows, width), jnp.bfloat16)
    vmem = pl.BlockSpec(memory_space=pltpu.VMEM)
    return pl.pallas_call(
        functools.partial(down_kernel, len(hidden), len(weights), order),
        in_specs=[pl.BlockSpec(memory_space=pltpu.SMEM)] + [vmem] * (len(hidden) + len(weights)),
        out_specs=[vmem, vmem],
        scratch_shapes=[pltpu.VMEM((rows, units), jnp.bfloat16)],
        out_shape=[out, out],
        compiler_params=pltpu.CompilerParams(vmem_limit_bytes=6 * MIB),
        cost_estimate=cost(),
        name="down",
    )(place.reshape(1), *hidden, *[in_vmem(w) for w in weights])


def add(a, b):
    return (a.astype(jnp.float32) + b.astype(jnp.float32)).astype(jnp.bfloat16)


def kernel_call(kernel, shapes, *operands, name, size=1024):
    vmem = pl.BlockSpec(memory_space=pltpu.VMEM)
    return pl.pallas_call(
        kernel,
        in_specs=[vmem] * len(operands),
        out_specs=[vmem] * len(shapes),
        out_shape=[jax.ShapeDtypeStruct(shape, jnp.bfloat16) for shape in shapes],
        compiler_params=pltpu.CompilerParams(vmem_limit_bytes=4 * MIB),
        cost_estimate=cost(size),
        name=name,
    )(*operands)


def tiles_of(width):
    return 256 if width % 256 == 0 else 128 if width % 128 == 0 else width


def add_halves_kernel(a_ref, *refs):
    piece_refs, (first_ref, second_ref) = refs[:-2], refs[-2:]
    half, rows, width = first_ref.shape[0], a_ref.shape[-2], a_ref.shape[-1]
    tile = tiles_of(width)

    def columns(j, carry):
        cols = pl.ds(pl.multiple_of(j * tile, tile), tile)
        top = 0
        for ref in piece_refs:
            size = ref.shape[0]
            i, s, row = top // (2 * rows), top // rows % 2, top % rows
            total = add(a_ref[i, s, row : row + size, cols], ref[:, cols])
            (first_ref if i < half else second_ref)[i % half, s, row : row + size, cols] = total
            top += size
        return carry

    lax.fori_loop(0, width // tile, columns, 0)


def add_halves(a, pieces):
    if a.shape[-1] % 128 or a.shape[-2] % 16:
        total = add(a, jnp.stack(pieces).reshape(a.shape))
        return total[: a.shape[0] // 2], total[a.shape[0] // 2 :]
    shape = (a.shape[0] // 2, *a.shape[1:])
    return kernel_call(add_halves_kernel, [shape, shape], a, *pieces, name="add_halves")


def gated_kernel(a_ref, b_ref, out_ref):
    width = out_ref.shape[-1]
    tile = tiles_of(width)

    def columns(j, carry):
        cols = pl.ds(pl.multiple_of(j * tile, tile), tile)
        gate, up = (a_ref[0, s, :, cols].astype(jnp.float32) + b_ref[0, s, :, cols].astype(jnp.float32) for s in (0, 1))
        out_ref[:, cols] = (gate / (1 + jnp.exp(-gate)) * up).astype(jnp.bfloat16)
        return carry

    lax.fori_loop(0, width // tile, columns, 0)


def gated_sum(a, b):
    if a.shape[-1] % 128 or a.shape[-2] % 16:
        gate, up = (a[0, s].astype(jnp.float32) + b[0, s].astype(jnp.float32) for s in (0, 1))
        return (jax.nn.silu(gate) * up).astype(jnp.bfloat16)
    return kernel_call(gated_kernel, [a.shape[2:]], a, b, name="gated", size=8 * MIB)[0]


def deal_kernel(edges, place_ref, x_ref, *out_refs):
    count = x_ref.shape[0]
    for i in range(count):
        source = place_ref[0] ^ reverse_bits(i, n_bits(count))
        for out_ref, lo, hi in zip(out_refs, edges, edges[1:]):
            out_ref[i] = x_ref[source, lo:hi]


def deal(place, x, edges):
    count, _, width = x.shape
    sizes = [hi - lo for lo, hi in zip(edges, edges[1:])]
    if width % 128 or any(size % 16 for size in sizes):
        x = jnp.take(x, place ^ reverse_bits(jnp.arange(count), n_bits(count)), axis=0)
        return [x[:, lo:hi] for lo, hi in zip(edges, edges[1:])]
    vmem = pl.BlockSpec(memory_space=pltpu.VMEM)
    return pl.pallas_call(
        functools.partial(deal_kernel, edges),
        in_specs=[pl.BlockSpec(memory_space=pltpu.SMEM), vmem],
        out_specs=[vmem] * len(sizes),
        out_shape=[jax.ShapeDtypeStruct((count, size, width), x.dtype) for size in sizes],
        compiler_params=pltpu.CompilerParams(vmem_limit_bytes=4 * MIB),
        cost_estimate=cost(),
        name="deal",
    )(place.reshape(1), x)


def collect_kernel(edges, place_ref, *refs):
    part_refs, out_ref = refs[:-1], refs[-1]
    count = out_ref.shape[0]
    pieces = [ref.at[m] for ref in part_refs for m in range(ref.shape[0])]
    for i in range(count):
        target = place_ref[0] ^ reverse_bits(i, n_bits(count))
        for piece, lo, hi in zip(pieces, edges, edges[1:]):
            out_ref[target, lo:hi] = piece[i]


def collect(place, parts, edges):
    _, count, _, width = parts[0].shape
    if width % 128 or any((hi - lo) % 16 for lo, hi in zip(edges, edges[1:])):
        order = reverse_bits(place ^ jnp.arange(count), n_bits(count))
        return jnp.take(jnp.concatenate([piece for part in parts for piece in part], axis=1), order, axis=0)
    vmem = pl.BlockSpec(memory_space=pltpu.VMEM)
    return pl.pallas_call(
        functools.partial(collect_kernel, edges),
        in_specs=[pl.BlockSpec(memory_space=pltpu.SMEM)] + [vmem] * len(parts),
        out_specs=vmem,
        out_shape=jax.ShapeDtypeStruct((count, edges[-1], width), parts[0].dtype),
        compiler_params=pltpu.CompilerParams(vmem_limit_bytes=4 * MIB),
        cost_estimate=cost(),
        name="collect",
    )(place.reshape(1), *parts)


def on_device(n_wide, n_nar, cuts, tokens, gw, gs, uw, us, dw, ds):
    wide, nar = lax.axis_index("wide"), lax.axis_index("nar")
    nar_bits, wide_bits = n_bits(n_nar), n_bits(n_wide)
    rows, width = tokens.shape
    fast = width % 128 == 0
    n = len(cuts)
    edges = [sum(cuts[:k]) // n_nar for k in range(n + 1)]
    dealt = deal(nar, after(tokens.reshape(n_nar, rows // n_nar, width), wide), edges)
    tok = [[t.reshape(1, -1, width)] for t in dealt]
    level = [wide_bits] * n

    def gather_tokens(k, to, *others):
        while level[k] > to:
            level[k] -= 1
            got = flip(tok[k][0], "wide", n_wide, 1 << level[k])
            if others:
                got = after(got, *others)
            tok[k] = [jnp.concatenate([tok[k][0], got])] if level[k] else [tok[k][0], got]

    def sum_core(k, pieces=8):
        for b in range(nar_bits - 1):
            flat = send[k].reshape(-1, send[k].shape[-1])
            size = min(max(flat.shape[0] // pieces, 16), send[k].shape[-2])
            got = [flip(flat[i : i + size], "nar", n_nar, 1 << b) for i in range(0, flat.shape[0], size)]
            keep[k], send[k] = add_halves(keep[k], got)

    far = 1 << (nar_bits - 1)

    def gated(k, *others):
        got = after(flip(send[k], "nar", n_nar, far), *others)
        hidden[k] = [gated_sum(keep[k], got)]
        hidden[k].append(flip(hidden[k][0], "nar", n_nar, far))

    def gather_hidden(k, pieces=1):
        for b in reversed(range(nar_bits - 1)):
            cut = [piece for g in hidden[k] for piece in jnp.split(g, pieces)]
            hidden[k] = hidden[k] + [flip(g, "nar", n_nar, 1 << b) for g in cut]

    keep, send, hidden = [None] * n, [None] * n, [None] * n
    parts, todo = [None] * n, [0] * n
    orders = [tuple(range(wide_bits)) if k != 2 or wide_bits < 2 else (1, 0, *range(2, wide_bits)) for k in range(n)]

    def scatter(k, to, *others, split=False):
        while todo[k] > to:
            mask = 1 << orders[k][wide_bits - todo[k]]
            todo[k] -= 1
            mine, other = parts[k]
            half = mine.shape[0] // 2
            if todo[k] and split:
                got = [flip(other[:half], "wide", n_wide, mask), flip(other[half:], "wide", n_wide, mask)]
                got = [after(g, *others) if others else g for g in got]
                parts[k] = (add(mine[:half], got[0]), add(mine[half:], got[1]))
            else:
                got = flip(other, "wide", n_wide, mask)
                total = add(mine, after(got, *others) if others else got)
                parts[k] = (total[:half], total[half:]) if todo[k] else (total,)

    def products(k, *others):
        keep[k], send[k] = gate_up(wide, [after(tok[k][0], *others), *tok[k][1:]], gate, up, n_nar)

    def finish(k, weights, *others):
        chunks = k if isinstance(k, list) else [k]
        rows_of = [g for j in chunks for g in hidden[j]]
        rows_of[0] = after(rows_of[0], *others)
        k = chunks[0]
        parts[k], todo[k] = down(wide, rows_of, weights, n_wide, orders[k]), wide_bits

    if not fast or n != 4 or wide_bits < 2:
        gate, up, down_w = [decode(gw, gs)], [decode(uw, us)], [decode(dw, ds)]
        for k in range(n):
            gather_tokens(k, 0)
            products(k)
            sum_core(k)
            gated(k)
            gather_hidden(k)
            finish(k, down_w)
            scatter(k, 0)
    else:
        gate = [decode_part(after(gw, dealt[0]), gs, 0, 2)]
        for k in (0, 1):
            gather_tokens(k, wide_bits - 1, gate[0])
        gate.append(decode_part(after(gw, gate[0], tok[0][0]), gs, 1, 2))
        for k in (2, 3):
            tok[k] = [after(tok[k][0], tok[0][0])]
        for k in (0, 1):
            gather_tokens(k, 1, gate[1])
        up = [decode_part(after(uw, tok[0][0], tok[1][0]), us, 0, 1)]
        for k in (2, 3):
            gather_tokens(k, wide_bits - 1, up[0])
        gather_tokens(0, 0, up[0])
        products(0)
        for k in (2, 3):
            gather_tokens(k, 1, send[0])
        gather_tokens(1, 0, send[0])
        send[0] = after(send[0], tok[1][1], tok[2][0], tok[3][0])
        tok[2], tok[3] = [after(tok[2][0], send[0])], [after(tok[3][0], send[0])]
        gather_tokens(2, 0)
        gather_tokens(3, 0)
        sum_core(0, 4)
        down_w = []
        for k in range(3):
            products(k + 1, send[0] if k == 0 else hidden[k - 1][0])
            if k < 2:
                tok[k + 2][1] = after(tok[k + 2][1], send[k + 1])
                send[k + 1] = after(send[k + 1], tok[k + 2][1])
            sum_core(k + 1)
            others = [send[k + 1]]
            if k > 0:
                down_w.append(decode_part(after(dw, send[k + 1]), ds, k - 1, 2))
                others += [down_w[-1], hidden[k - 1][1]]
            gated(k, *others)
        for j in (0, 1):
            hidden[j] = [after(g, hidden[2][0]) for g in hidden[j]]
            gather_hidden(j, 1)
        finish([0, 1], down_w, hidden[2][0])
        gated(3, parts[0][1])
        gather_hidden(2, 2)
        finish(2, down_w, hidden[3][0])
        scatter(0, wide_bits - 1, parts[2][1], split=True)
        gather_hidden(3, 1)
        finish(3, down_w, *parts[0])
        scatter(0, wide_bits - 2, parts[3][1])
        scatter(2, wide_bits - 1, parts[3][1])
        scatter(3, wide_bits - 1)
        for k in (0, 2):
            parts[k] = tuple(after(p, parts[3][1]) for p in parts[k])
        for k in (3, 0, 2):
            scatter(k, 0)
        parts = [parts[0], parts[2], parts[3]]
    outs = [part[0].reshape(-1, n_nar, cuts[0] // n_nar, width) for part in parts]
    return collect(nar, outs, edges).reshape(rows, width)


def solution(mesh):
    n_wide, n_nar = mesh.shape["wide"], mesh.shape["nar"]

    def local(tokens, *weights):
        rows = tokens.shape[0]
        cuts = (128,) * (rows // 128) if rows % 128 == 0 and 128 // n_nar >= 16 else (rows,)
        return on_device(n_wide, n_nar, cuts, tokens, *weights)

    in_specs = (
        P("grp", ("nar", "wide")),
        P("nar", "wide"),
        P("nar", "wide"),
        P("nar", "wide"),
        P("nar", "wide"),
        P("wide", "nar"),
        P("wide", "nar"),
    )
    return jax.shard_map(
        local, mesh=mesh, in_specs=in_specs, out_specs=P("grp", ("nar", "wide")), check_vma=False
    )
```

```python
import functools

import jax
import jax.numpy as jnp
from jax import lax
from jax.experimental import pallas as pl
from jax.experimental.pallas import tpu as pltpu
from jax.sharding import PartitionSpec as P

GROUP = 128
MIB = 1 << 20


def n_bits(size):
    return size.bit_length() - 1


def reverse_bits(value, bits):
    out = value * 0
    for b in range(bits):
        out = out + ((value >> b) & 1) * (1 << (bits - 1 - b))
    return out


def spread(value, order):
    return sum(((value >> (len(order) - 1 - s)) & 1) << b for s, b in enumerate(order))


def flip(array, axis, size, mask):
    return lax.ppermute(array, axis, [(i, i ^ mask) for i in range(size)])


def decode(codes, scales):
    rows, cols = codes.shape
    blocks = codes.reshape(rows // GROUP, GROUP, cols) * scales.astype(jnp.bfloat16)[:, None, :]
    return blocks.reshape(rows, cols)


def in_hbm(array):
    return pltpu.with_memory_space_constraint(array, pltpu.HBM)


def in_vmem(array):
    return pltpu.with_memory_space_constraint(array, pltpu.VMEM)


def after(array, *others):
    return lax.optimization_barrier((array, *others))[0]


def cost(size=1024):
    return pl.CostEstimate(flops=size, bytes_accessed=size, transcendentals=0)


def decode_kernel(first, block, w_ref, sc_ref, out_ref, scale_ref, arrived, scaled):
    size = out_ref.shape[0]
    scales = pltpu.make_async_copy(sc_ref, scale_ref, scaled)

    def fetch(k):
        return pltpu.make_async_copy(
            w_ref.at[pl.ds(first + k * block, block)], out_ref.at[pl.ds(k * block, block)], arrived.at[k]
        )

    count = size // block
    scales.start()
    for k in range(count):
        fetch(k).start()
    scales.wait()
    for k in range(count):
        fetch(k).wait()
        for g in range(k * block // GROUP, (k + 1) * block // GROUP):
            rows = slice(g * GROUP, (g + 1) * GROUP)
            scale = scale_ref[first // GROUP + g : first // GROUP + g + 1]
            out_ref[rows] = out_ref[rows] * scale.astype(jnp.bfloat16)


def decode_part(codes, scales, part, parts):
    depth, units = codes.shape
    size = depth // parts
    block = 256 if size % 256 == 0 else GROUP
    hbm = pl.BlockSpec(memory_space=pl.ANY)
    return pl.pallas_call(
        functools.partial(decode_kernel, part * size, block),
        in_specs=[hbm, hbm],
        out_specs=pl.BlockSpec(memory_space=pltpu.VMEM),
        out_shape=pltpu.VMEM((size, units), jnp.bfloat16),
        scratch_shapes=[
            pltpu.VMEM(scales.shape, jnp.float32),
            pltpu.SemaphoreType.DMA((size // block,)),
            pltpu.SemaphoreType.DMA,
        ],
        compiler_params=pltpu.CompilerParams(vmem_limit_bytes=6 * MIB),
        cost_estimate=cost(),
        name="decode",
    )(in_hbm(codes), in_hbm(scales))


def gate_up_kernel(n_tok, n_gate, n_up, place_ref, *refs):
    cuts = (n_tok, n_tok + n_gate, n_tok + n_gate + n_up)
    tok_refs, gate_refs, up_refs = refs[: cuts[0]], refs[cuts[0] : cuts[1]], refs[cuts[1] : cuts[2]]
    keep_ref, send_ref, x_ref = refs[cuts[2] :]
    shards = [ref.at[i] for ref in tok_refs for i in range(ref.shape[0])]
    bits = n_bits(len(shards))
    for p, shard in enumerate(shards):
        width = shard.shape[1]
        spot = pl.multiple_of((place_ref[0] ^ reverse_bits(p, bits)) * width, width)
        x_ref[:, pl.ds(spot, width)] = shard[...]
    half, quarter = keep_ref.shape[0], keep_ref.shape[2]
    units = gate_refs[0].shape[1]
    tile = 256 if units % 256 == 0 else 128

    def column(j, carry):
        cols = pl.ds(pl.multiple_of(j * tile, tile), tile)
        for s, w_refs in enumerate((gate_refs, up_refs)):
            part = sum(
                jnp.dot(
                    x_ref[:, k * w_ref.shape[0] : (k + 1) * w_ref.shape[0]],
                    w_ref[:, cols],
                    preferred_element_type=jnp.float32,
                )
                for k, w_ref in enumerate(w_refs)
            ).astype(jnp.bfloat16)
            for b in range(half):
                keep_ref[b, s, :, cols] = part[b * quarter : (b + 1) * quarter]
                send_ref[b, s, :, cols] = part[(half + b) * quarter : (half + b + 1) * quarter]
        return carry

    lax.fori_loop(0, units // tile, column, 0)


def gate_up(place, shards, gate, up, n_nar):
    count, (rows, width) = sum(t.shape[0] for t in shards), shards[0].shape[1:]
    depth, units = sum(g.shape[0] for g in gate), gate[0].shape[1]
    quarter = rows // n_nar
    shape = (n_nar // 2, 2, quarter, units)
    if width % 128:
        order = reverse_bits(place ^ jnp.arange(count), n_bits(count))
        x = jnp.take(jnp.concatenate(shards), order, axis=0).transpose(1, 0, 2).reshape(rows, depth)
        both = [
            jnp.dot(x, jnp.concatenate(w), preferred_element_type=jnp.float32)
            .astype(jnp.bfloat16)
            .reshape(2, n_nar // 2, quarter, units)
            for w in (gate, up)
        ]
        both = jnp.stack(both, axis=2)
        return both[0], both[1]
    out = jax.ShapeDtypeStruct(shape, jnp.bfloat16)
    vmem = pl.BlockSpec(memory_space=pltpu.VMEM)
    return pl.pallas_call(
        functools.partial(gate_up_kernel, len(shards), len(gate), len(up)),
        in_specs=[pl.BlockSpec(memory_space=pltpu.SMEM)] + [vmem] * (len(shards) + len(gate) + len(up)),
        out_specs=[vmem, vmem],
        scratch_shapes=[pltpu.VMEM((rows, depth), jnp.bfloat16)],
        out_shape=[out, out],
        compiler_params=pltpu.CompilerParams(vmem_limit_bytes=6 * MIB),
        cost_estimate=cost(),
        name="gate_up",
    )(place.reshape(1), *shards, *[in_vmem(w) for w in (*gate, *up)])


def down_kernel(parts, pieces, order, place_ref, *refs):
    h_refs, w_refs, (keep_ref, send_ref, h_ref) = refs[:parts], refs[parts : parts + pieces], refs[parts + pieces :]
    top = 0
    for ref in h_refs:
        h_ref[top : top + ref.shape[0]] = ref[...]
        top += ref.shape[0]
    half, _, width = keep_ref.shape
    size = w_refs[0].shape[0]
    for out_ref, first in ((send_ref, half), (keep_ref, 0)):

        def block(i, carry, out_ref=out_ref, first=first):
            spot = pl.multiple_of((place_ref[0] ^ spread(first + i, order)) * width, width)
            part = sum(
                jnp.dot(
                    h_ref[:, k * size : (k + 1) * size], w_ref[:, pl.ds(spot, width)], preferred_element_type=jnp.float32
                )
                for k, w_ref in enumerate(w_refs)
            )
            out_ref[i] = part.astype(jnp.bfloat16)
            return carry

        lax.fori_loop(0, half, block, 0)


def down(place, hidden, weights, n_wide, order):
    rows = sum(h.shape[0] for h in hidden)
    units, features = sum(w.shape[0] for w in weights), weights[0].shape[1]
    width, half = features // n_wide, n_wide // 2
    if width % 128:
        part = jnp.dot(jnp.concatenate(hidden), jnp.concatenate(weights), preferred_element_type=jnp.float32)
        part = part.astype(jnp.bfloat16).reshape(rows, n_wide, width).transpose(1, 0, 2)
        part = jnp.take(part, place ^ spread(jnp.arange(n_wide), order), axis=0)
        return part[:half], part[half:]
    out = jax.ShapeDtypeStruct((half, rows, width), jnp.bfloat16)
    vmem = pl.BlockSpec(memory_space=pltpu.VMEM)
    return pl.pallas_call(
        functools.partial(down_kernel, len(hidden), len(weights), order),
        in_specs=[pl.BlockSpec(memory_space=pltpu.SMEM)] + [vmem] * (len(hidden) + len(weights)),
        out_specs=[vmem, vmem],
        scratch_shapes=[pltpu.VMEM((rows, units), jnp.bfloat16)],
        out_shape=[out, out],
        compiler_params=pltpu.CompilerParams(vmem_limit_bytes=6 * MIB),
        cost_estimate=cost(),
        name="down",
    )(place.reshape(1), *hidden, *[in_vmem(w) for w in weights])


def add(a, b):
    return (a.astype(jnp.float32) + b.astype(jnp.float32)).astype(jnp.bfloat16)


def kernel_call(kernel, shapes, *operands, name, size=1024):
    vmem = pl.BlockSpec(memory_space=pltpu.VMEM)
    return pl.pallas_call(
        kernel,
        in_specs=[vmem] * len(operands),
        out_specs=[vmem] * len(shapes),
        out_shape=[jax.ShapeDtypeStruct(shape, jnp.bfloat16) for shape in shapes],
        compiler_params=pltpu.CompilerParams(vmem_limit_bytes=4 * MIB),
        cost_estimate=cost(size),
        name=name,
    )(*operands)


def tiles_of(width):
    return 256 if width % 256 == 0 else 128 if width % 128 == 0 else width


def add_halves_kernel(a_ref, *refs):
    piece_refs, (first_ref, second_ref) = refs[:-2], refs[-2:]
    half, rows, width = first_ref.shape[0], a_ref.shape[-2], a_ref.shape[-1]
    tile = tiles_of(width)

    def columns(j, carry):
        cols = pl.ds(pl.multiple_of(j * tile, tile), tile)
        top = 0
        for ref in piece_refs:
            size = ref.shape[0]
            i, s, row = top // (2 * rows), top // rows % 2, top % rows
            total = add(a_ref[i, s, row : row + size, cols], ref[:, cols])
            (first_ref if i < half else second_ref)[i % half, s, row : row + size, cols] = total
            top += size
        return carry

    lax.fori_loop(0, width // tile, columns, 0)


def add_halves(a, pieces):
    if a.shape[-1] % 128 or a.shape[-2] % 16:
        total = add(a, jnp.stack(pieces).reshape(a.shape))
        return total[: a.shape[0] // 2], total[a.shape[0] // 2 :]
    shape = (a.shape[0] // 2, *a.shape[1:])
    return kernel_call(add_halves_kernel, [shape, shape], a, *pieces, name="add_halves")


def gated_kernel(a_ref, b_ref, out_ref):
    width = out_ref.shape[-1]
    tile = tiles_of(width)

    def columns(j, carry):
        cols = pl.ds(pl.multiple_of(j * tile, tile), tile)
        gate, up = (a_ref[0, s, :, cols].astype(jnp.float32) + b_ref[0, s, :, cols].astype(jnp.float32) for s in (0, 1))
        out_ref[:, cols] = (gate / (1 + jnp.exp(-gate)) * up).astype(jnp.bfloat16)
        return carry

    lax.fori_loop(0, width // tile, columns, 0)


def gated_sum(a, b):
    if a.shape[-1] % 128 or a.shape[-2] % 16:
        gate, up = (a[0, s].astype(jnp.float32) + b[0, s].astype(jnp.float32) for s in (0, 1))
        return (jax.nn.silu(gate) * up).astype(jnp.bfloat16)
    return kernel_call(gated_kernel, [a.shape[2:]], a, b, name="gated", size=8 * MIB)[0]


def deal_kernel(edges, place_ref, x_ref, *out_refs):
    count = x_ref.shape[0]
    for i in range(count):
        source = place_ref[0] ^ reverse_bits(i, n_bits(count))
        for out_ref, lo, hi in zip(out_refs, edges, edges[1:]):
            out_ref[i] = x_ref[source, lo:hi]


def deal(place, x, edges):
    count, _, width = x.shape
    sizes = [hi - lo for lo, hi in zip(edges, edges[1:])]
    if width % 128 or any(size % 16 for size in sizes):
        x = jnp.take(x, place ^ reverse_bits(jnp.arange(count), n_bits(count)), axis=0)
        return [x[:, lo:hi] for lo, hi in zip(edges, edges[1:])]
    vmem = pl.BlockSpec(memory_space=pltpu.VMEM)
    return pl.pallas_call(
        functools.partial(deal_kernel, edges),
        in_specs=[pl.BlockSpec(memory_space=pltpu.SMEM), vmem],
        out_specs=[vmem] * len(sizes),
        out_shape=[jax.ShapeDtypeStruct((count, size, width), x.dtype) for size in sizes],
        compiler_params=pltpu.CompilerParams(vmem_limit_bytes=4 * MIB),
        cost_estimate=cost(),
        name="deal",
    )(place.reshape(1), x)


def collect_kernel(edges, place_ref, *refs):
    part_refs, out_ref = refs[:-1], refs[-1]
    count = out_ref.shape[0]
    pieces = [ref.at[m] for ref in part_refs for m in range(ref.shape[0])]
    for i in range(count):
        target = place_ref[0] ^ reverse_bits(i, n_bits(count))
        for piece, lo, hi in zip(pieces, edges, edges[1:]):
            out_ref[target, lo:hi] = piece[i]


def collect(place, parts, edges):
    _, count, _, width = parts[0].shape
    if width % 128 or any((hi - lo) % 16 for lo, hi in zip(edges, edges[1:])):
        order = reverse_bits(place ^ jnp.arange(count), n_bits(count))
        return jnp.take(jnp.concatenate([piece for part in parts for piece in part], axis=1), order, axis=0)
    vmem = pl.BlockSpec(memory_space=pltpu.VMEM)
    return pl.pallas_call(
        functools.partial(collect_kernel, edges),
        in_specs=[pl.BlockSpec(memory_space=pltpu.SMEM)] + [vmem] * len(parts),
        out_specs=vmem,
        out_shape=jax.ShapeDtypeStruct((count, edges[-1], width), parts[0].dtype),
        compiler_params=pltpu.CompilerParams(vmem_limit_bytes=4 * MIB),
        cost_estimate=cost(),
        name="collect",
    )(place.reshape(1), *parts)


def on_device(n_wide, n_nar, cuts, tokens, gw, gs, uw, us, dw, ds):
    wide, nar = lax.axis_index("wide"), lax.axis_index("nar")
    nar_bits, wide_bits = n_bits(n_nar), n_bits(n_wide)
    rows, width = tokens.shape
    fast = width % 128 == 0
    n = len(cuts)
    edges = [sum(cuts[:k]) // n_nar for k in range(n + 1)]
    dealt = deal(nar, after(tokens.reshape(n_nar, rows // n_nar, width), wide), edges)
    tok = [[t.reshape(1, -1, width)] for t in dealt]
    level = [wide_bits] * n

    def gather_tokens(k, to, *others):
        while level[k] > to:
            level[k] -= 1
            got = flip(tok[k][0], "wide", n_wide, 1 << level[k])
            if others:
                got = after(got, *others)
            tok[k] = [jnp.concatenate([tok[k][0], got])] if level[k] else [tok[k][0], got]

    def sum_core(k, pieces=8):
        for b in range(nar_bits - 1):
            flat = send[k].reshape(-1, send[k].shape[-1])
            size = min(max(flat.shape[0] // pieces, 16), send[k].shape[-2])
            got = [flip(flat[i : i + size], "nar", n_nar, 1 << b) for i in range(0, flat.shape[0], size)]
            keep[k], send[k] = add_halves(keep[k], got)

    far = 1 << (nar_bits - 1)

    def gated(k, *others):
        got = after(flip(send[k], "nar", n_nar, far), *others)
        hidden[k] = [gated_sum(keep[k], got)]
        hidden[k].append(flip(hidden[k][0], "nar", n_nar, far))

    def gather_hidden(k, pieces=1):
        for b in reversed(range(nar_bits - 1)):
            cut = [piece for g in hidden[k] for piece in jnp.split(g, pieces)]
            hidden[k] = hidden[k] + [flip(g, "nar", n_nar, 1 << b) for g in cut]

    keep, send, hidden = [None] * n, [None] * n, [None] * n
    parts, todo = [None] * n, [0] * n
    orders = [tuple(range(wide_bits)) if k != 2 or wide_bits < 2 else (1, 0, *range(2, wide_bits)) for k in range(n)]

    def scatter(k, to, *others, split=False):
        while todo[k] > to:
            mask = 1 << orders[k][wide_bits - todo[k]]
            todo[k] -= 1
            mine, other = parts[k]
            half = mine.shape[0] // 2
            if todo[k] and split:
                got = [flip(other[:half], "wide", n_wide, mask), flip(other[half:], "wide", n_wide, mask)]
                got = [after(g, *others) if others else g for g in got]
                parts[k] = (add(mine[:half], got[0]), add(mine[half:], got[1]))
            else:
                got = flip(other, "wide", n_wide, mask)
                total = add(mine, after(got, *others) if others else got)
                parts[k] = (total[:half], total[half:]) if todo[k] else (total,)

    def products(k, *others):
        keep[k], send[k] = gate_up(wide, [after(tok[k][0], *others), *tok[k][1:]], gate, up, n_nar)

    def finish(k, weights, *others):
        chunks = k if isinstance(k, list) else [k]
        rows_of = [g for j in chunks for g in hidden[j]]
        rows_of[0] = after(rows_of[0], *others)
        k = chunks[0]
        parts[k], todo[k] = down(wide, rows_of, weights, n_wide, orders[k]), wide_bits

    if not fast or n != 4 or wide_bits < 2:
        gate, up, down_w = [decode(gw, gs)], [decode(uw, us)], [decode(dw, ds)]
        for k in range(n):
            gather_tokens(k, 0)
            products(k)
            sum_core(k)
            gated(k)
            gather_hidden(k)
            finish(k, down_w)
            scatter(k, 0)
    else:
        gate = [decode_part(after(gw, dealt[0]), gs, 0, 2)]
        for k in (0, 1):
            gather_tokens(k, wide_bits - 1, gate[0])
        gate.append(decode_part(after(gw, gate[0], tok[0][0]), gs, 1, 2))
        for k in (2, 3):
            tok[k] = [after(tok[k][0], gate[1])]
        for k in (0, 1):
            gather_tokens(k, 1, gate[1])
        up = [decode_part(after(uw, tok[0][0], tok[1][0]), us, 0, 1)]
        for k in (2, 3):
            gather_tokens(k, wide_bits - 1, up[0])
        gather_tokens(0, 0, up[0])
        products(0)
        for k in (2, 3):
            gather_tokens(k, 1, send[0])
        gather_tokens(1, 0, send[0])
        send[0] = after(send[0], tok[1][1], tok[2][0], tok[3][0])
        tok[2], tok[3] = [after(tok[2][0], send[0])], [after(tok[3][0], send[0])]
        gather_tokens(2, 0)
        gather_tokens(3, 0)
        sum_core(0, 4)
        down_w = []
        for k in range(3):
            products(k + 1, send[0] if k == 0 else hidden[k - 1][0])
            if k < 2:
                tok[k + 2][1] = after(tok[k + 2][1], send[k + 1])
                send[k + 1] = after(send[k + 1], tok[k + 2][1])
            sum_core(k + 1)
            others = [send[k + 1]]
            if k > 0:
                down_w.append(decode_part(after(dw, send[k + 1]), ds, k - 1, 2))
                others += [down_w[-1], hidden[k - 1][1]]
            gated(k, *others)
        for j in (0, 1):
            hidden[j] = [after(g, hidden[2][0]) for g in hidden[j]]
            gather_hidden(j, 2)
        finish([0, 1], down_w, hidden[2][0])
        gated(3, parts[0][1])
        gather_hidden(2, 1)
        finish(2, down_w, hidden[3][0])
        hidden[3][1] = after(hidden[3][1], parts[2][1])
        gather_hidden(3, 2)
        finish(3, down_w, parts[2][1])
        scatter(0, wide_bits - 1, parts[3][1], split=True)
        scatter(2, wide_bits - 1, parts[3][1])
        scatter(0, wide_bits - 2)
        scatter(3, wide_bits - 1)
        for k in (0, 2):
            parts[k] = tuple(after(p, parts[3][1]) for p in parts[k])
        for k in (3, 0, 2):
            scatter(k, 0)
        parts = [parts[0], parts[2], parts[3]]
    outs = [part[0].reshape(-1, n_nar, cuts[0] // n_nar, width) for part in parts]
    return collect(nar, outs, edges).reshape(rows, width)


def solution(mesh):
    n_wide, n_nar = mesh.shape["wide"], mesh.shape["nar"]

    def local(tokens, *weights):
        rows = tokens.shape[0]
        cuts = (128,) * (rows // 128) if rows % 128 == 0 and 128 // n_nar >= 16 else (rows,)
        return on_device(n_wide, n_nar, cuts, tokens, *weights)

    in_specs = (
        P("grp", ("nar", "wide")),
        P("nar", "wide"),
        P("nar", "wide"),
        P("nar", "wide"),
        P("nar", "wide"),
        P("wide", "nar"),
        P("wide", "nar"),
    )
    return jax.shard_map(
        local, mesh=mesh, in_specs=in_specs, out_specs=P("grp", ("nar", "wide")), check_vma=False
    )
```

```python
import functools

import jax
import jax.numpy as jnp
from jax import lax
from jax.experimental import pallas as pl
from jax.experimental.pallas import tpu as pltpu
from jax.sharding import PartitionSpec as P

GROUP = 128
MIB = 1 << 20


def n_bits(size):
    return size.bit_length() - 1


def reverse_bits(value, bits):
    out = value * 0
    for b in range(bits):
        out = out + ((value >> b) & 1) * (1 << (bits - 1 - b))
    return out


def spread(value, order):
    return sum(((value >> (len(order) - 1 - s)) & 1) << b for s, b in enumerate(order))


def flip(array, axis, size, mask):
    return lax.ppermute(array, axis, [(i, i ^ mask) for i in range(size)])


def decode(codes, scales):
    rows, cols = codes.shape
    blocks = codes.reshape(rows // GROUP, GROUP, cols) * scales.astype(jnp.bfloat16)[:, None, :]
    return blocks.reshape(rows, cols)


def in_hbm(array):
    return pltpu.with_memory_space_constraint(array, pltpu.HBM)


def in_vmem(array):
    return pltpu.with_memory_space_constraint(array, pltpu.VMEM)


def after(array, *others):
    return lax.optimization_barrier((array, *others))[0]


def cost(size=1024):
    return pl.CostEstimate(flops=size, bytes_accessed=size, transcendentals=0)


def decode_kernel(first, block, w_ref, sc_ref, out_ref, scale_ref, arrived, scaled):
    size = out_ref.shape[0]
    scales = pltpu.make_async_copy(sc_ref, scale_ref, scaled)

    def fetch(k):
        return pltpu.make_async_copy(
            w_ref.at[pl.ds(first + k * block, block)], out_ref.at[pl.ds(k * block, block)], arrived.at[k]
        )

    count = size // block
    scales.start()
    for k in range(count):
        fetch(k).start()
    scales.wait()
    for k in range(count):
        fetch(k).wait()
        for g in range(k * block // GROUP, (k + 1) * block // GROUP):
            rows = slice(g * GROUP, (g + 1) * GROUP)
            scale = scale_ref[first // GROUP + g : first // GROUP + g + 1]
            out_ref[rows] = out_ref[rows] * scale.astype(jnp.bfloat16)


def decode_part(codes, scales, part, parts):
    depth, units = codes.shape
    size = depth // parts
    block = 256 if size % 256 == 0 else GROUP
    hbm = pl.BlockSpec(memory_space=pl.ANY)
    return pl.pallas_call(
        functools.partial(decode_kernel, part * size, block),
        in_specs=[hbm, hbm],
        out_specs=pl.BlockSpec(memory_space=pltpu.VMEM),
        out_shape=pltpu.VMEM((size, units), jnp.bfloat16),
        scratch_shapes=[
            pltpu.VMEM(scales.shape, jnp.float32),
            pltpu.SemaphoreType.DMA((size // block,)),
            pltpu.SemaphoreType.DMA,
        ],
        compiler_params=pltpu.CompilerParams(vmem_limit_bytes=6 * MIB),
        cost_estimate=cost(),
        name="decode",
    )(in_hbm(codes), in_hbm(scales))


def gate_up_kernel(n_tok, n_gate, n_up, place_ref, *refs):
    cuts = (n_tok, n_tok + n_gate, n_tok + n_gate + n_up)
    tok_refs, gate_refs, up_refs = refs[: cuts[0]], refs[cuts[0] : cuts[1]], refs[cuts[1] : cuts[2]]
    keep_ref, send_ref, x_ref = refs[cuts[2] :]
    shards = [ref.at[i] for ref in tok_refs for i in range(ref.shape[0])]
    bits = n_bits(len(shards))
    for p, shard in enumerate(shards):
        width = shard.shape[1]
        spot = pl.multiple_of((place_ref[0] ^ reverse_bits(p, bits)) * width, width)
        x_ref[:, pl.ds(spot, width)] = shard[...]
    half, quarter = keep_ref.shape[0], keep_ref.shape[2]
    units = gate_refs[0].shape[1]
    tile = 256 if units % 256 == 0 else 128

    def column(j, carry):
        cols = pl.ds(pl.multiple_of(j * tile, tile), tile)
        for s, w_refs in enumerate((gate_refs, up_refs)):
            part = sum(
                jnp.dot(
                    x_ref[:, k * w_ref.shape[0] : (k + 1) * w_ref.shape[0]],
                    w_ref[:, cols],
                    preferred_element_type=jnp.float32,
                )
                for k, w_ref in enumerate(w_refs)
            ).astype(jnp.bfloat16)
            for b in range(half):
                keep_ref[b, s, :, cols] = part[b * quarter : (b + 1) * quarter]
                send_ref[b, s, :, cols] = part[(half + b) * quarter : (half + b + 1) * quarter]
        return carry

    lax.fori_loop(0, units // tile, column, 0)


def gate_up(place, shards, gate, up, n_nar):
    count, (rows, width) = sum(t.shape[0] for t in shards), shards[0].shape[1:]
    depth, units = sum(g.shape[0] for g in gate), gate[0].shape[1]
    quarter = rows // n_nar
    shape = (n_nar // 2, 2, quarter, units)
    if width % 128:
        order = reverse_bits(place ^ jnp.arange(count), n_bits(count))
        x = jnp.take(jnp.concatenate(shards), order, axis=0).transpose(1, 0, 2).reshape(rows, depth)
        both = [
            jnp.dot(x, jnp.concatenate(w), preferred_element_type=jnp.float32)
            .astype(jnp.bfloat16)
            .reshape(2, n_nar // 2, quarter, units)
            for w in (gate, up)
        ]
        both = jnp.stack(both, axis=2)
        return both[0], both[1]
    out = jax.ShapeDtypeStruct(shape, jnp.bfloat16)
    vmem = pl.BlockSpec(memory_space=pltpu.VMEM)
    return pl.pallas_call(
        functools.partial(gate_up_kernel, len(shards), len(gate), len(up)),
        in_specs=[pl.BlockSpec(memory_space=pltpu.SMEM)] + [vmem] * (len(shards) + len(gate) + len(up)),
        out_specs=[vmem, vmem],
        scratch_shapes=[pltpu.VMEM((rows, depth), jnp.bfloat16)],
        out_shape=[out, out],
        compiler_params=pltpu.CompilerParams(vmem_limit_bytes=6 * MIB),
        cost_estimate=cost(),
        name="gate_up",
    )(place.reshape(1), *shards, *[in_vmem(w) for w in (*gate, *up)])


def down_kernel(parts, pieces, order, place_ref, *refs):
    h_refs, w_refs, (keep_ref, send_ref, h_ref) = refs[:parts], refs[parts : parts + pieces], refs[parts + pieces :]
    top = 0
    for ref in h_refs:
        h_ref[top : top + ref.shape[0]] = ref[...]
        top += ref.shape[0]
    half, _, width = keep_ref.shape
    size = w_refs[0].shape[0]
    for out_ref, first in ((send_ref, half), (keep_ref, 0)):

        def block(i, carry, out_ref=out_ref, first=first):
            spot = pl.multiple_of((place_ref[0] ^ spread(first + i, order)) * width, width)
            part = sum(
                jnp.dot(
                    h_ref[:, k * size : (k + 1) * size], w_ref[:, pl.ds(spot, width)], preferred_element_type=jnp.float32
                )
                for k, w_ref in enumerate(w_refs)
            )
            out_ref[i] = part.astype(jnp.bfloat16)
            return carry

        lax.fori_loop(0, half, block, 0)


def down(place, hidden, weights, n_wide, order):
    rows = sum(h.shape[0] for h in hidden)
    units, features = sum(w.shape[0] for w in weights), weights[0].shape[1]
    width, half = features // n_wide, n_wide // 2
    if width % 128:
        part = jnp.dot(jnp.concatenate(hidden), jnp.concatenate(weights), preferred_element_type=jnp.float32)
        part = part.astype(jnp.bfloat16).reshape(rows, n_wide, width).transpose(1, 0, 2)
        part = jnp.take(part, place ^ spread(jnp.arange(n_wide), order), axis=0)
        return part[:half], part[half:]
    out = jax.ShapeDtypeStruct((half, rows, width), jnp.bfloat16)
    vmem = pl.BlockSpec(memory_space=pltpu.VMEM)
    return pl.pallas_call(
        functools.partial(down_kernel, len(hidden), len(weights), order),
        in_specs=[pl.BlockSpec(memory_space=pltpu.SMEM)] + [vmem] * (len(hidden) + len(weights)),
        out_specs=[vmem, vmem],
        scratch_shapes=[pltpu.VMEM((rows, units), jnp.bfloat16)],
        out_shape=[out, out],
        compiler_params=pltpu.CompilerParams(vmem_limit_bytes=6 * MIB),
        cost_estimate=cost(),
        name="down",
    )(place.reshape(1), *hidden, *[in_vmem(w) for w in weights])


def add(a, b):
    return (a.astype(jnp.float32) + b.astype(jnp.float32)).astype(jnp.bfloat16)


def kernel_call(kernel, shapes, *operands, name, size=1024):
    vmem = pl.BlockSpec(memory_space=pltpu.VMEM)
    return pl.pallas_call(
        kernel,
        in_specs=[vmem] * len(operands),
        out_specs=[vmem] * len(shapes),
        out_shape=[jax.ShapeDtypeStruct(shape, jnp.bfloat16) for shape in shapes],
        compiler_params=pltpu.CompilerParams(vmem_limit_bytes=4 * MIB),
        cost_estimate=cost(size),
        name=name,
    )(*operands)


def tiles_of(width):
    return 256 if width % 256 == 0 else 128 if width % 128 == 0 else width


def add_halves_kernel(a_ref, *refs):
    piece_refs, (first_ref, second_ref) = refs[:-2], refs[-2:]
    half, rows, width = first_ref.shape[0], a_ref.shape[-2], a_ref.shape[-1]
    tile = tiles_of(width)

    def columns(j, carry):
        cols = pl.ds(pl.multiple_of(j * tile, tile), tile)
        top = 0
        for ref in piece_refs:
            size = ref.shape[0]
            i, s, row = top // (2 * rows), top // rows % 2, top % rows
            total = add(a_ref[i, s, row : row + size, cols], ref[:, cols])
            (first_ref if i < half else second_ref)[i % half, s, row : row + size, cols] = total
            top += size
        return carry

    lax.fori_loop(0, width // tile, columns, 0)


def add_halves(a, pieces):
    if a.shape[-1] % 128 or a.shape[-2] % 16:
        total = add(a, jnp.stack(pieces).reshape(a.shape))
        return total[: a.shape[0] // 2], total[a.shape[0] // 2 :]
    shape = (a.shape[0] // 2, *a.shape[1:])
    return kernel_call(add_halves_kernel, [shape, shape], a, *pieces, name="add_halves")


def gated_kernel(a_ref, b_ref, out_ref):
    width = out_ref.shape[-1]
    tile = tiles_of(width)

    def columns(j, carry):
        cols = pl.ds(pl.multiple_of(j * tile, tile), tile)
        gate, up = (a_ref[0, s, :, cols].astype(jnp.float32) + b_ref[0, s, :, cols].astype(jnp.float32) for s in (0, 1))
        out_ref[:, cols] = (gate / (1 + jnp.exp(-gate)) * up).astype(jnp.bfloat16)
        return carry

    lax.fori_loop(0, width // tile, columns, 0)


def gated_sum(a, b):
    if a.shape[-1] % 128 or a.shape[-2] % 16:
        gate, up = (a[0, s].astype(jnp.float32) + b[0, s].astype(jnp.float32) for s in (0, 1))
        return (jax.nn.silu(gate) * up).astype(jnp.bfloat16)
    return kernel_call(gated_kernel, [a.shape[2:]], a, b, name="gated", size=8 * MIB)[0]


def deal_kernel(edges, place_ref, x_ref, *out_refs):
    count = x_ref.shape[0]
    for i in range(count):
        source = place_ref[0] ^ reverse_bits(i, n_bits(count))
        for out_ref, lo, hi in zip(out_refs, edges, edges[1:]):
            out_ref[i] = x_ref[source, lo:hi]


def deal(place, x, edges):
    count, _, width = x.shape
    sizes = [hi - lo for lo, hi in zip(edges, edges[1:])]
    if width % 128 or any(size % 16 for size in sizes):
        x = jnp.take(x, place ^ reverse_bits(jnp.arange(count), n_bits(count)), axis=0)
        return [x[:, lo:hi] for lo, hi in zip(edges, edges[1:])]
    vmem = pl.BlockSpec(memory_space=pltpu.VMEM)
    return pl.pallas_call(
        functools.partial(deal_kernel, edges),
        in_specs=[pl.BlockSpec(memory_space=pltpu.SMEM), vmem],
        out_specs=[vmem] * len(sizes),
        out_shape=[jax.ShapeDtypeStruct((count, size, width), x.dtype) for size in sizes],
        compiler_params=pltpu.CompilerParams(vmem_limit_bytes=4 * MIB),
        cost_estimate=cost(),
        name="deal",
    )(place.reshape(1), x)


def collect_kernel(edges, place_ref, *refs):
    part_refs, out_ref = refs[:-1], refs[-1]
    count = out_ref.shape[0]
    pieces = [ref.at[m] for ref in part_refs for m in range(ref.shape[0])]
    for i in range(count):
        target = place_ref[0] ^ reverse_bits(i, n_bits(count))
        for piece, lo, hi in zip(pieces, edges, edges[1:]):
            out_ref[target, lo:hi] = piece[i]


def collect(place, parts, edges):
    _, count, _, width = parts[0].shape
    if width % 128 or any((hi - lo) % 16 for lo, hi in zip(edges, edges[1:])):
        order = reverse_bits(place ^ jnp.arange(count), n_bits(count))
        return jnp.take(jnp.concatenate([piece for part in parts for piece in part], axis=1), order, axis=0)
    vmem = pl.BlockSpec(memory_space=pltpu.VMEM)
    return pl.pallas_call(
        functools.partial(collect_kernel, edges),
        in_specs=[pl.BlockSpec(memory_space=pltpu.SMEM)] + [vmem] * len(parts),
        out_specs=vmem,
        out_shape=jax.ShapeDtypeStruct((count, edges[-1], width), parts[0].dtype),
        compiler_params=pltpu.CompilerParams(vmem_limit_bytes=4 * MIB),
        cost_estimate=cost(),
        name="collect",
    )(place.reshape(1), *parts)


def on_device(n_wide, n_nar, cuts, tokens, gw, gs, uw, us, dw, ds):
    wide, nar = lax.axis_index("wide"), lax.axis_index("nar")
    nar_bits, wide_bits = n_bits(n_nar), n_bits(n_wide)
    rows, width = tokens.shape
    fast = width % 128 == 0
    n = len(cuts)
    edges = [sum(cuts[:k]) // n_nar for k in range(n + 1)]
    dealt = deal(nar, after(tokens.reshape(n_nar, rows // n_nar, width), wide), edges)
    tok = [[t.reshape(1, -1, width)] for t in dealt]
    level = [wide_bits] * n

    def gather_tokens(k, to, *others):
        while level[k] > to:
            level[k] -= 1
            got = flip(tok[k][0], "wide", n_wide, 1 << level[k])
            if others:
                got = after(got, *others)
            tok[k] = [jnp.concatenate([tok[k][0], got])] if level[k] else [tok[k][0], got]

    def sum_core(k, pieces=8):
        for b in range(nar_bits - 1):
            flat = send[k].reshape(-1, send[k].shape[-1])
            size = min(max(flat.shape[0] // pieces, 16), send[k].shape[-2])
            got = [flip(flat[i : i + size], "nar", n_nar, 1 << b) for i in range(0, flat.shape[0], size)]
            keep[k], send[k] = add_halves(keep[k], got)

    far = 1 << (nar_bits - 1)

    def gated(k, *others):
        got = after(flip(send[k], "nar", n_nar, far), *others)
        hidden[k] = [gated_sum(keep[k], got)]
        hidden[k].append(flip(hidden[k][0], "nar", n_nar, far))

    def gather_hidden(k, pieces=1):
        for b in reversed(range(nar_bits - 1)):
            cut = [piece for g in hidden[k] for piece in jnp.split(g, pieces)]
            hidden[k] = hidden[k] + [flip(g, "nar", n_nar, 1 << b) for g in cut]

    keep, send, hidden = [None] * n, [None] * n, [None] * n
    parts, todo = [None] * n, [0] * n
    orders = [tuple(range(wide_bits)) if k != 2 or wide_bits < 2 else (1, 0, *range(2, wide_bits)) for k in range(n)]

    def scatter(k, to, *others, split=False):
        while todo[k] > to:
            mask = 1 << orders[k][wide_bits - todo[k]]
            todo[k] -= 1
            mine, other = parts[k]
            half = mine.shape[0] // 2
            if todo[k] and split:
                got = [flip(other[:half], "wide", n_wide, mask), flip(other[half:], "wide", n_wide, mask)]
                got = [after(g, *others) if others else g for g in got]
                parts[k] = (add(mine[:half], got[0]), add(mine[half:], got[1]))
            else:
                got = flip(other, "wide", n_wide, mask)
                total = add(mine, after(got, *others) if others else got)
                parts[k] = (total[:half], total[half:]) if todo[k] else (total,)

    def products(k, *others):
        keep[k], send[k] = gate_up(wide, [after(tok[k][0], *others), *tok[k][1:]], gate, up, n_nar)

    def finish(k, weights, *others):
        chunks = k if isinstance(k, list) else [k]
        rows_of = [g for j in chunks for g in hidden[j]]
        rows_of[0] = after(rows_of[0], *others)
        k = chunks[0]
        parts[k], todo[k] = down(wide, rows_of, weights, n_wide, orders[k]), wide_bits

    if not fast or n != 4 or wide_bits < 2:
        gate, up, down_w = [decode(gw, gs)], [decode(uw, us)], [decode(dw, ds)]
        for k in range(n):
            gather_tokens(k, 0)
            products(k)
            sum_core(k)
            gated(k)
            gather_hidden(k)
            finish(k, down_w)
            scatter(k, 0)
    else:
        gate = [decode_part(after(gw, dealt[0]), gs, 0, 2)]
        for k in (0, 1):
            gather_tokens(k, wide_bits - 1, gate[0])
        gate.append(decode_part(after(gw, gate[0], tok[0][0]), gs, 1, 2))
        for k in (2, 3):
            tok[k] = [after(tok[k][0], gate[1])]
        gather_tokens(0, 1, gate[1])
        up = [decode_part(after(uw, tok[0][0]), us, 0, 1)]
        gather_tokens(1, 1, up[0])
        for k in (2, 3):
            gather_tokens(k, wide_bits - 1, up[0])
        gather_tokens(0, 0, up[0])
        products(0)
        for k in (2, 3):
            gather_tokens(k, 1, send[0])
        gather_tokens(1, 0, send[0])
        send[0] = after(send[0], tok[1][1], tok[2][0], tok[3][0])
        tok[2], tok[3] = [after(tok[2][0], send[0])], [after(tok[3][0], send[0])]
        gather_tokens(2, 0)
        gather_tokens(3, 0)
        sum_core(0, 4)
        down_w = []
        for k in range(3):
            products(k + 1, send[0] if k == 0 else hidden[k - 1][0])
            if k < 2:
                tok[k + 2][1] = after(tok[k + 2][1], send[k + 1])
                send[k + 1] = after(send[k + 1], tok[k + 2][1])
            sum_core(k + 1)
            others = [send[k + 1]]
            if k > 0:
                down_w.append(decode_part(after(dw, send[k + 1]), ds, k - 1, 2))
                others += [down_w[-1], hidden[k - 1][1]]
            gated(k, *others)
        for j in (0, 1):
            hidden[j] = [after(g, hidden[2][0]) for g in hidden[j]]
            gather_hidden(j, 2)
        finish([0, 1], down_w, hidden[2][0])
        gated(3, parts[0][1])
        gather_hidden(2, 1)
        finish(2, down_w, hidden[3][0])
        hidden[3][1] = after(hidden[3][1], parts[2][1])
        gather_hidden(3, 2)
        finish(3, down_w, parts[2][1])
        scatter(0, wide_bits - 1, parts[3][1], split=True)
        scatter(2, wide_bits - 1, parts[3][1])
        scatter(0, wide_bits - 2)
        scatter(3, wide_bits - 1)
        for k in (0, 2):
            parts[k] = tuple(after(p, parts[3][1]) for p in parts[k])
        for k in (3, 0, 2):
            scatter(k, 0)
        parts = [parts[0], parts[2], parts[3]]
    outs = [part[0].reshape(-1, n_nar, cuts[0] // n_nar, width) for part in parts]
    return collect(nar, outs, edges).reshape(rows, width)


def solution(mesh):
    n_wide, n_nar = mesh.shape["wide"], mesh.shape["nar"]

    def local(tokens, *weights):
        rows = tokens.shape[0]
        cuts = (128,) * (rows // 128) if rows % 128 == 0 and 128 // n_nar >= 16 else (rows,)
        return on_device(n_wide, n_nar, cuts, tokens, *weights)

    in_specs = (
        P("grp", ("nar", "wide")),
        P("nar", "wide"),
        P("nar", "wide"),
        P("nar", "wide"),
        P("nar", "wide"),
        P("wide", "nar"),
        P("wide", "nar"),
    )
    return jax.shard_map(
        local, mesh=mesh, in_specs=in_specs, out_specs=P("grp", ("nar", "wide")), check_vma=False
    )
```
